32 devices in a mesh: dense: 16 (over z, x, core), attn: 2 (over y).
Axes of the slice: x: 2, y: 2, z: 4, core: 2. Of those that a mesh axis runs over, the one named last changes fastest.
Arguments:
- queries: bfloat16 [4096, 4096], P('dense', 'attn'), may hold values from -30 to 30
- keys: bfloat16 [4096, 1024], P('dense', 'attn'), may hold values from -13 to 13
- values: bfloat16 [4096, 1024], P('dense', 'attn'), may hold values from -24 to 24
- segments: int32 [4096], replicated, may hold values from 0 to 5, never falling along the last dimension, each value on 1 to 2048 neighbouring positions
- out_weight: bfloat16 [4096, 4096], P('attn', 'dense'), may hold values from -0.09375 to 0.09375
Outputs:
- projected: bfloat16 [4096, 4096], P('dense', 'attn')
The draws below stay inside these ranges and needn't reach their ends.
All inputs are finite; a program needn't handle non-finite values.
Results may differ from the reference program's by a relative error of at most 0.012.
Values may be sent and summed in bfloat16 or wider, within the bound.
No kernel may reach another device: no remote copies, remote signals or barrier semaphores. Data moves between devices by JAX's collectives and lax.ppermute only.
A program may use at most 128 MiB of HBM per device.

```python
import math
import jax
import jax.numpy as jnp
import numpy as np
from jax import lax

D = 4096
QUERY_HEAD_COUNT = 32
KEY_VALUE_HEADS = 8
HEAD_WIDTH = 128
DOCS = 6
WINDOW_TOKENS = 4096


def draw_queries(key, part):
    base_offset = jax.random.normal(jax.random.fold_in(key, 601), (WINDOW_TOKENS, QUERY_HEAD_COUNT * HEAD_WIDTH), jnp.float32)
    queries = 1.5 * jnp.clip(base_offset, -5.0, 5.0)
    return queries.astype(jnp.bfloat16)


def draw_keys(key, part):
    base_offset = jax.random.normal(jax.random.fold_in(key, 701), (WINDOW_TOKENS, KEY_VALUE_HEADS * HEAD_WIDTH), jnp.float32)
    keys = jnp.clip(base_offset, -5.0, 5.0)
    return keys.astype(jnp.bfloat16)


def level_of(key, extent, cuts, low, high):
    def one(dim, shards_of):
        steps = jax.random.uniform(jax.random.fold_in(jax.random.fold_in(key, 6), dim), (shards_of,), jnp.float32, low / len(cuts), high / len(cuts))
        return jnp.repeat(jnp.exp(steps), extent[dim] // shards_of).reshape((-1,) + (1,) * (len(extent) - dim - 1))

    level = one(*cuts[0])
    for cut in cuts[1:]:
        level = level * one(*cut)
    return level


def profile(number_of, total, most, lean):
    portions = [(1 << 20) // math.isqrt(rank ** lean) + 1 for rank in range(2, number_of + 1)]
    rest, counts = total - most - (number_of - 1), [1] * (number_of - 1)
    while rest > 0:
        movable = [i for i in range(number_of - 1) if counts[i] < most]
        mass, budget = sum([portions[i] for i in movable]), rest
        for i in movable:
            addition = min(most - counts[i], max(1, budget * portions[i] // mass), rest)
            counts[i] = counts[i] + addition
            rest = rest - addition
    return np.array([most] + counts)


def ragged(rng, amount, total, bound, lean):
    if amount == 2:
        one = jax.random.randint(rng, (), max(1, total - bound), min(bound, total - 1) + 1)
        return jnp.stack([one, total - one])
    sizes = jnp.asarray(profile(amount, total, bound, lean), jnp.int32)
    pairs = (amount - 1) // 2
    source_of, sink = sizes[1:1 + 2 * pairs:2], sizes[2:2 + 2 * pairs:2]
    slack = jnp.minimum(source_of - 1, bound - sink)
    passed = jax.random.randint(jax.random.fold_in(rng, 1), (pairs,), 0, 1 << 20) % (slack + 1)
    sizes = sizes.at[1:1 + 2 * pairs:2].set(source_of - passed).at[2:2 + 2 * pairs:2].set(sink + passed)
    return sizes[jax.random.permutation(jax.random.fold_in(rng, 2), amount)]


def noise(rng, shape, deviation, most, split=(), kind=jnp.bfloat16):
    factor_of = level_of(rng, shape, split, -0.22, 0.18) if split else 1.0
    result = jax.random.normal(rng, shape, jnp.float32) * deviation * factor_of
    return jnp.minimum(jnp.maximum(result, -most), most).astype(kind)


def setup_inputs(seed: int = 0) -> dict:
    key_list = jax.random.split(jax.random.key(seed), 6)
    queries = draw_queries(jax.random.fold_in(key_list[5], 71), 0)
    keys = draw_keys(jax.random.fold_in(key_list[5], 71), 0)
    values = noise(key_list[2], (WINDOW_TOKENS, KEY_VALUE_HEADS * HEAD_WIDTH), 4.0, 24.0, ((0, 16), (1, 2)))
    segments = jnp.searchsorted(jnp.cumsum(ragged(key_list[3], DOCS, WINDOW_TOKENS, WINDOW_TOKENS // 2, 2)), jnp.arange(WINDOW_TOKENS), side="right").astype(jnp.int32)
    out_weight = noise(key_list[4], (QUERY_HEAD_COUNT * HEAD_WIDTH, D), (QUERY_HEAD_COUNT * HEAD_WIDTH) ** -0.5, 0.09375, ((0, 2), (1, 16)))
    return {"queries": queries, "keys": keys, "values": values, "segments": segments, "out_weight": out_weight}


NEGATIVE = -1e+30

def reference(queries, keys, values, segments, out_weight):
    head_group = QUERY_HEAD_COUNT // KEY_VALUE_HEADS
    inv_root = 1.0 / math.sqrt(HEAD_WIDTH)
    rows_block = min(1024, WINDOW_TOKENS)
    blocks_count = WINDOW_TOKENS // rows_block
    positions = jnp.arange(WINDOW_TOKENS, dtype=jnp.int32)
    query_split = queries.reshape(blocks_count, rows_block, QUERY_HEAD_COUNT, HEAD_WIDTH)

    def one_task(task):
        head = task // blocks_count
        which = task % blocks_count
        sliced = lax.dynamic_index_in_dim(query_split, which, 0, keepdims=False)
        query_head = lax.dynamic_index_in_dim(sliced, head, 1, keepdims=False)
        column = (head // head_group * HEAD_WIDTH).astype(jnp.int32)
        key_head = lax.dynamic_slice_in_dim(keys, column, HEAD_WIDTH, 1)
        value_head = lax.dynamic_slice_in_dim(values, column, HEAD_WIDTH, 1)
        lower = (which * rows_block).astype(jnp.int32)
        query_pos = lower + jnp.arange(rows_block, dtype=jnp.int32)
        query_docs = lax.dynamic_slice_in_dim(segments, lower, rows_block)
        visible = (query_docs[:, None] == segments[None, :]) & (positions[None, :] <= query_pos[:, None])
        scores = jnp.dot(query_head, key_head.T, preferred_element_type=jnp.float32) * inv_root
        scores = jnp.where(visible, scores, NEGATIVE)
        row_max = lax.optimization_barrier(jnp.max(scores, axis=-1))
        expd = jnp.where(visible, jnp.exp(scores - row_max[:, None]), 0.0)
        totals = lax.optimization_barrier(jnp.sum(expd, axis=-1))
        mixed = jnp.dot(expd.astype(jnp.bfloat16), value_head, preferred_element_type=jnp.float32) / totals[:, None]
        return mixed.astype(jnp.bfloat16)
    results = lax.map(one_task, jnp.arange(QUERY_HEAD_COUNT * blocks_count, dtype=jnp.int32))
    attended = results.reshape(QUERY_HEAD_COUNT, blocks_count, rows_block, HEAD_WIDTH).transpose(1, 2, 0, 3).reshape(WINDOW_TOKENS, QUERY_HEAD_COUNT * HEAD_WIDTH)
    return jnp.dot(attended, out_weight, preferred_element_type=jnp.float32).astype(jnp.bfloat16)
```

```python
import functools
import math

import jax
import jax.numpy as jnp
import numpy as np
from jax import lax
from jax.experimental import pallas as pl
from jax.experimental.pallas import tpu as pltpu
from jax.sharding import PartitionSpec as P

HEAD = 128
NEGATIVE = -1e30
AXES = ("dense", "attn")
ANY = pl.BlockSpec(memory_space=pl.ANY)
SMEM = pl.BlockSpec(memory_space=pltpu.SMEM)
VMEM = pl.BlockSpec(memory_space=pltpu.VMEM)


def xor(a, b):
    return lax.bitwise_xor(a, jnp.int32(b))


def params(mib):
    return pltpu.CompilerParams(vmem_limit_bytes=mib * 2**20)


def split_kv_kernel(group, meta_ref, k_ref, v_ref, *outs):
    g = lax.rem(meta_ref[0], group)
    for k in range(group):
        at = pl.ds(pl.multiple_of(xor(g, k) * HEAD, HEAD), HEAD)
        outs[k][:, :HEAD] = k_ref[:, at]
        outs[k][:, HEAD:] = v_ref[:, at]


def split_q_kernel(group, meta_ref, q_ref, *outs):
    g = lax.rem(meta_ref[0], group)
    width = outs[0].shape[1]
    for k in range(group):
        outs[k][...] = q_ref[:, pl.ds(pl.multiple_of(xor(g, k) * width, width), width)]


def attention_kernel(group, hops, heads, meta_ref, seg_ref, segrow_ref, *refs):
    n_kv = (hops + 1) * group
    q_refs, kv_refs = refs[:group], refs[group : group + n_kv]
    out_refs = refs[group + n_kv : group + n_kv + 2]
    q_s, k_s, v_s, s_s, m_s, l_s, acc_s, seg_s, sem = refs[group + n_kv + 2 :]
    n = q_s.shape[2]
    copies = []
    for k in range(group):
        for h in range(heads):
            copies.append((q_refs[k].at[:, pl.ds(h * HEAD, HEAD)], q_s.at[k, h]))
    for i in range(n_kv):
        copies.append((kv_refs[i].at[:, pl.ds(0, HEAD)], k_s.at[i]))
        copies.append((kv_refs[i].at[:, pl.ds(HEAD, HEAD)], v_s.at[i]))
    copies = [pltpu.make_async_copy(a, b, sem.at[i]) for i, (a, b) in enumerate(copies)]
    for c in copies:
        c.start()
    for c in copies:
        c.wait()

    device = meta_ref[0]
    plane, g = device // group, lax.rem(device, group)
    scale = math.log2(math.e) / math.sqrt(HEAD)
    lanes = n // HEAD

    def piece(i):
        return (plane - i // group) * group + lax.bitwise_xor(g, lax.rem(i, group))

    def one_query_piece(k, carry):
        qp = plane * group + lax.bitwise_xor(g, k)
        q_first, q_last = seg_ref[qp * n], seg_ref[qp * n + n - 1]
        row = segrow_ref[pl.ds(qp, 1), :].astype(jnp.float32)
        seg_s[...] = jnp.broadcast_to(row, (HEAD, n)).T
        m_s[...] = jnp.full(m_s.shape, NEGATIVE, jnp.float32)
        l_s[...] = jnp.zeros(l_s.shape, jnp.float32)
        acc_s[...] = jnp.zeros(acc_s.shape, jnp.float32)

        def state(i):
            kp = piece(i)
            safe = jnp.maximum(kp, 0)
            active = (kp >= 0) & (kp <= qp) & (seg_ref[safe * n + n - 1] >= q_first)
            whole = (kp < qp) & (seg_ref[safe * n] == q_last)
            return kp, safe, active, whole

        def score(i, carry):
            kp, safe, active, whole = state(i)

            def scores(h):
                return lax.dot_general(
                    q_s[k, h], k_s[i], (((1,), (1,)), ((), ())), preferred_element_type=jnp.float32
                )

            def keep(h, parts):
                best = m_s[h]
                for t, part in enumerate(parts):
                    s_s[i, h, :, t * HEAD : (t + 1) * HEAD] = part
                    best = jnp.maximum(best, part)
                m_s[h] = best

            @pl.when(active & whole)
            def _():
                for h in range(heads):
                    s = scores(h)
                    keep(h, [s[:, t * HEAD : (t + 1) * HEAD] for t in range(lanes)])

            @pl.when(active & jnp.logical_not(whole))
            def _():
                seg_k = segrow_ref[pl.ds(safe, 1), :].astype(jnp.float32)
                ahead = lax.broadcasted_iota(jnp.int32, (n, HEAD), 1) - lax.broadcasted_iota(
                    jnp.int32, (n, HEAD), 0
                )
                seen = [
                    (ahead + t * HEAD <= (qp - kp) * n)
                    & (seg_s[...] == seg_k[:, t * HEAD : (t + 1) * HEAD])
                    for t in range(lanes)
                ]
                for h in range(heads):
                    s = scores(h)
                    keep(
                        h,
                        [
                            jnp.where(seen[t], s[:, t * HEAD : (t + 1) * HEAD], NEGATIVE)
                            for t in range(lanes)
                        ],
                    )

            return carry

        lax.fori_loop(0, n_kv, score, 0)
        for h in range(heads):
            m_s[h] = jnp.broadcast_to(jnp.max(m_s[h], axis=1, keepdims=True), (n, HEAD))

        def mix(i, carry):
            active = state(i)[2]

            @pl.when(active)
            def _():
                for h in range(heads):
                    top = m_s[h]
                    parts = [
                        jnp.exp2((s_s[i, h, :, t * HEAD : (t + 1) * HEAD] - top) * scale)
                        for t in range(lanes)
                    ]
                    l_s[h] += functools.reduce(jnp.add, parts)
                    weights = jnp.concatenate([p.astype(jnp.bfloat16) for p in parts], axis=1)
                    acc_s[h] += jnp.dot(weights, v_s[i], preferred_element_type=jnp.float32)

            return carry

        lax.fori_loop(0, n_kv, mix, 0)
        half = heads // 2
        for h in range(heads):
            total = jnp.sum(l_s[h], axis=1, keepdims=True)
            out_refs[h // half][k, :, (h % half) * HEAD : (h % half + 1) * HEAD] = (
                acc_s[h] / total
            ).astype(jnp.bfloat16)
        return carry

    lax.fori_loop(0, group, one_query_piece, 0)


def project_kernel(group, attn, cands, sel_at, meta_ref, *refs):
    n_w = len(cands) * attn
    w_refs = [refs[c * attn : (c + 1) * attn] for c in range(len(cands))]
    a_refs = refs[n_w : n_w + 2 * group * attn]
    out_refs = refs[n_w + 2 * group * attn : n_w + 2 * group * attn + group * attn]
    a_s, w_s, a_sem, w_sem = refs[n_w + 3 * group * attn :]
    g = lax.rem(meta_ref[0], group)
    n, width = a_refs[0].shape[1], a_refs[0].shape[2] * 2
    half = width // 2

    def w_copy(c, to, m, j):
        rows = pl.ds(pl.multiple_of(xor(g, j) * width, width), width)
        return pltpu.make_async_copy(
            w_refs[c][m].at[rows, :], w_s.at[to, pl.ds((m * group + j) * width, width), :], w_sem.at[to]
        )

    def each_w(act):
        for to in range(attn):
            for c, code in enumerate(cands):

                @pl.when(meta_ref[sel_at + to] == code)
                def _(c=c, to=to):
                    for m in range(attn):
                        for j in range(group):
                            act(w_copy(c, to, m, j))

    def a_copies(k):
        found = []
        for m in range(attn):
            for j in range(group):
                for part in range(2):
                    at = (m * group + j) * width + part * half
                    found.append(
                        pltpu.make_async_copy(
                            a_refs[(m * group + j) * 2 + part].at[j ^ k],
                            a_s.at[k, :, pl.ds(at, half)],
                            a_sem.at[k],
                        )
                    )
        return found

    each_w(lambda copy: copy.start())
    for k in range(group):
        for copy in a_copies(k):
            copy.start()
    each_w(lambda copy: copy.wait())
    cols = w_s.shape[2]
    for k in range(group):
        for copy in a_copies(k):
            copy.wait()
        if cols % HEAD == 0:
            weights = jnp.concatenate([w_s[to] for to in range(attn)], axis=1)
            found = jnp.dot(a_s[k], weights, preferred_element_type=jnp.float32)
            for to in range(attn):
                out_refs[to * group + k][...] = found[:, to * cols : (to + 1) * cols].astype(jnp.bfloat16)
        else:
            for to in range(attn):
                out_refs[to * group + k][...] = jnp.dot(
                    a_s[k], w_s[to], preferred_element_type=jnp.float32
                ).astype(jnp.bfloat16)


def place_kernel(group, attn, rounds, zz_at, meta_ref, y_ref, *refs):
    out_ref = refs[-1]
    g, y = lax.rem(meta_ref[0], group), y_ref[0]
    cols = refs[0].shape[1]
    for r in range(rounds):
        for m in range(attn):
            for k in range(group):
                at = ((meta_ref[zz_at + r] * group + xor(g, k)) * attn + xor(y, m)) * cols
                out_ref[:, pl.ds(pl.multiple_of(at, cols), cols)] = refs[(r * attn + m) * group + k][...]


def schedule(planes, attn):
    rounds = planes // attn
    table = np.zeros((planes, rounds, attn), np.int64)
    for z in range(planes):
        for y in range(attn):
            blocks = range(y * rounds, (y + 1) * rounds)
            table[z, :, y] = sorted(blocks, key=lambda b: (abs(b - z), b))
    return table


def code_of(z, block, planes):
    return z - block if block <= z else planes - 1 + block - z


def shards(dense, attn, queries, keys, values, segments, out_weight):
    n = queries.shape[0]
    tokens = segments.shape[0]
    group = keys.shape[1] // HEAD
    heads = queries.shape[1] // HEAD // group
    width = heads * HEAD
    planes = dense // group
    rounds = planes // attn
    hops = min(-(-(tokens // 2 - 1) // (n * group)), planes - 1)
    cols = out_weight.shape[1] // attn

    def number(z, g, y):
        return (z * group + g) * attn + y

    def pairs(move):
        found = []
        for z in range(planes):
            for g in range(group):
                for y in range(attn):
                    to = move(z, g, y)
                    if 0 <= to[0] < planes:
                        found.append((number(z, g, y), number(*to)))
        return found

    def across(array, j, m):
        return lax.ppermute(array, AXES, pairs(lambda z, g, y: (z, g ^ j, y ^ m)))

    def up(array):
        return lax.ppermute(array, AXES, pairs(lambda z, g, y: (z + 1, g, y)))

    def down(array):
        return lax.ppermute(array, AXES, pairs(lambda z, g, y: (z - 1, g, y)))

    order = schedule(planes, attn)
    length = rounds * attn + rounds
    table = np.zeros((planes, attn, length), np.int32)
    cands = [set() for _ in range(rounds)]
    for z in range(planes):
        for y in range(attn):
            for r in range(rounds):
                for m in range(attn):
                    code = code_of(z, int(order[z, r, y ^ m]), planes)
                    table[z, y, r * attn + m] = code
                    cands[r].add(code)
                table[z, y, rounds * attn + r] = order[z, r, y] - y * rounds
    device = lax.axis_index("dense").astype(jnp.int32)
    y_here = lax.axis_index("attn").astype(jnp.int32)
    row = lax.dynamic_index_in_dim(
        jnp.asarray(table.reshape(planes * attn, length)), device // group * attn + y_here, 0, keepdims=False
    )
    meta = jnp.concatenate([device[None], row])
    y_meta = y_here[None]

    kv = pl.pallas_call(
        functools.partial(split_kv_kernel, group),
        out_shape=[jax.ShapeDtypeStruct((n, 2 * HEAD), jnp.bfloat16)] * group,
        in_specs=[SMEM, VMEM, VMEM],
        out_specs=[VMEM] * group,
        name="split_kv",
    )(meta, keys, values)
    kv = [kv[0]] + [across(kv[j], j, 0) for j in range(1, group)]
    all_kv = list(kv)
    for _ in range(hops):
        kv = [up(piece) for piece in kv]
        all_kv += kv

    q = pl.pallas_call(
        functools.partial(split_q_kernel, group),
        out_shape=[jax.ShapeDtypeStruct((n, width), jnp.bfloat16)] * group,
        in_specs=[SMEM, VMEM],
        out_specs=[VMEM] * group,
        name="split_q",
    )(meta, queries)
    q = [q[0]] + [across(q[j], j, 0) for j in range(1, group)]

    own = []
    for m in range(attn):
        part = lax.dynamic_slice_in_dim(out_weight, lax.bitwise_xor(y_here, jnp.int32(m)) * cols, cols, 1)
        own.append(part if m == 0 else across(part, 0, m))
    blocks = {0: own}
    here = own
    for s in range(1, planes):
        here = [down(part) for part in here]
        blocks[planes - 1 + s] = here
    tied = lax.optimization_barrier(tuple(own) + tuple(all_kv[-group:]))
    here = list(tied[:attn])
    all_kv[-group:] = tied[attn:]
    for s in range(1, planes):
        here = [up(part) for part in here]
        blocks[s] = here

    n_kv = (hops + 1) * group
    n_copies = group * heads + 2 * n_kv
    attended = pl.pallas_call(
        functools.partial(attention_kernel, group, hops, heads),
        out_shape=[jax.ShapeDtypeStruct((group, n, width // 2), jnp.bfloat16)] * 2,
        in_specs=[SMEM, SMEM, VMEM] + [ANY] * (group + n_kv),
        out_specs=[VMEM] * 2,
        scratch_shapes=[
            pltpu.VMEM((group, heads, n, HEAD), jnp.bfloat16),
            pltpu.VMEM((n_kv, n, HEAD), jnp.bfloat16),
            pltpu.VMEM((n_kv, n, HEAD), jnp.bfloat16),
            pltpu.VMEM((n_kv, heads, n, n), jnp.float32),
            pltpu.VMEM((heads, n, HEAD), jnp.float32),
            pltpu.VMEM((heads, n, HEAD), jnp.float32),
            pltpu.VMEM((heads, n, HEAD), jnp.float32),
            pltpu.VMEM((n, HEAD), jnp.float32),
            pltpu.SemaphoreType.DMA((n_copies,)),
        ],
        compiler_params=params(56),
        cost_estimate=pl.CostEstimate(
            flops=10 * 10**9, bytes_accessed=4 * 2**20, transcendentals=10**7
        ),
        name="attention",
    )(meta, segments, segments.reshape(dense, n), *q, *all_kv)

    gathered = {}
    for m in range(attn):
        for j in range(group):
            gathered[j, m] = [half if j == m == 0 else across(half, j, m) for half in attended]
    everything = [half for m in range(attn) for j in range(group) for half in gathered[j, m]]

    placed = []
    for r in range(rounds):
        codes = sorted(cands[r])
        found = pl.pallas_call(
            functools.partial(project_kernel, group, attn, codes, 1 + r * attn),
            out_shape=[jax.ShapeDtypeStruct((n, cols), jnp.bfloat16)] * (attn * group),
            in_specs=[SMEM] + [ANY] * (len(codes) * attn + 2 * group * attn),
            out_specs=[VMEM] * (attn * group),
            scratch_shapes=[
                pltpu.VMEM((group, n, attn * group * width), jnp.bfloat16),
                pltpu.VMEM((attn, attn * group * width, cols), jnp.bfloat16),
                pltpu.SemaphoreType.DMA((group,)),
                pltpu.SemaphoreType.DMA((attn,)),
            ],
            compiler_params=params(40),
            cost_estimate=pl.CostEstimate(
                flops=4 * 10**9, bytes_accessed=10 * 2**20, transcendentals=0
            ),
            name="project",
        )(meta, *[part for code in codes for part in blocks[code]], *everything)
        for m in range(attn):
            for k in range(group):
                piece = found[m * group + k]
                placed.append(piece if m == k == 0 else across(piece, k, m))

    if cols % HEAD == 0:
        return pl.pallas_call(
            functools.partial(place_kernel, group, attn, rounds, 1 + rounds * attn),
            out_shape=jax.ShapeDtypeStruct((n, rounds * group * attn * cols), jnp.bfloat16),
            in_specs=[SMEM, SMEM] + [VMEM] * len(placed),
            out_specs=VMEM,
            name="place",
        )(meta, y_meta, *placed)
    out = jnp.zeros((n, rounds * group * attn * cols), jnp.bfloat16)
    g = lax.rem(device, jnp.int32(group))
    for r in range(rounds):
        for m in range(attn):
            for k in range(group):
                at = ((meta[1 + rounds * attn + r] * group + xor(g, k)) * attn + xor(y_here, m)) * cols
                out = lax.dynamic_update_slice_in_dim(out, placed[(r * attn + m) * group + k], at, 1)
    return out


def solution(mesh):
    return jax.shard_map(
        functools.partial(shards, mesh.shape["dense"], mesh.shape["attn"]),
        mesh=mesh,
        in_specs=(
            P("dense", "attn"),
            P("dense", "attn"),
            P("dense", "attn"),
            P(),
            P("attn", "dense"),
        ),
        out_specs=P("dense", "attn"),
        check_vma=False,
    )
```

```python
import functools
import math

import jax
import jax.numpy as jnp
from jax import lax
from jax.experimental import pallas as pl
from jax.experimental.pallas import tpu as pltpu
from jax.sharding import PartitionSpec as P

HEAD = 128
NEGATIVE = -1e30
AXES = ("dense", "attn")
ANY = pl.BlockSpec(memory_space=pl.ANY)
SMEM = pl.BlockSpec(memory_space=pltpu.SMEM)
VMEM = pl.BlockSpec(memory_space=pltpu.VMEM)
LIGHT = pl.CostEstimate(flops=0, bytes_accessed=0, transcendentals=0)


def xor(a, b):
    return lax.bitwise_xor(a, jnp.int32(b))


def params(mib):
    return pltpu.CompilerParams(vmem_limit_bytes=mib * 2**20)


def place_in(group):
    device = lax.axis_index("dense").astype(jnp.int32)
    return device // group, lax.rem(device, jnp.int32(group)), lax.axis_index("attn").astype(jnp.int32)


def turn_of(z, y, planes, attn):
    return lax.bitwise_xor(z // (planes // attn), y)


def split_kv_kernel(group, *refs):
    g = place_in(group)[1]
    for core in range(2):
        k_ref, v_ref = refs[2 * core : 2 * core + 2]
        for o, out in enumerate(refs[4:]):
            at = pl.ds(pl.multiple_of(xor(g, 2 * o) * HEAD, HEAD), HEAD)
            out[core, :, :HEAD] = k_ref[:, at]
            out[core, :, HEAD:] = v_ref[:, at]


def split_q_kernel(group, *refs):
    g = place_in(group)[1]
    width = refs[2].shape[2]
    for core in range(2):
        for o, out in enumerate(refs[2:]):
            out[core] = refs[core][:, pl.ds(pl.multiple_of(xor(g, 2 * o) * width, width), width)]


def split_w_kernel(group, w_ref, *outs):
    g, y = place_in(group)[1:]
    rows, cols = outs[0].shape
    width = rows // group
    for m in range(len(outs)):
        at = pl.ds(pl.multiple_of(xor(y, m) * cols, cols), cols)
        for j in range(group):
            outs[m][j * width : (j + 1) * width, :] = w_ref[
                pl.ds(pl.multiple_of(xor(g, j) * width, width), width), at
            ]


def attention_kernel(group, heads, back, pairs, carried, final, seg_ref, segrow_ref, *refs):
    n_kv, n_q = len(back) * group, len(pairs) * 2
    refs = list(refs)
    take = lambda count: [refs.pop(0) for _ in range(count)]
    q_refs, kv_refs = take(len(pairs)), take(n_kv // 2)
    state_refs = [take(3) for _ in pairs] if carried else None
    out_refs = take(1 if final else 3)
    q_s, k_s, v_s, s_s, m_s, l_s, acc_s, seg_s, sem = refs
    n = segrow_ref.shape[1]
    rows = heads * n
    lanes = n // HEAD
    copies = []
    for k in range(n_q):
        for h in range(heads):
            q_part = q_refs[k // 2].at[k % 2, :, pl.ds(h * HEAD, HEAD)]
            copies.append((q_part, q_s.at[k, pl.ds(h * n, n), :]))
    for i in range(n_kv):
        kv = kv_refs[i // 2].at[i % 2]
        copies.append((kv.at[:, pl.ds(0, HEAD)], k_s.at[i]))
        copies.append((kv.at[:, pl.ds(HEAD, HEAD)], v_s.at[i]))
    copies = [pltpu.make_async_copy(a, b, sem.at[i]) for i, (a, b) in enumerate(copies)]
    for c in copies:
        c.start()
    for c in copies:
        c.wait()

    plane, g, _ = place_in(group)
    scale = math.log2(math.e) / math.sqrt(HEAD)

    def one_query_piece(pair, core, carry):
        at = 2 * pair + core
        given = [ref.at[core] for ref in state_refs[pair]] if carried else None
        qp = plane * group + lax.bitwise_xor(g, 2 * pairs[pair] + core)
        q_first, q_last = seg_ref[qp * n], seg_ref[qp * n + n - 1]

        def state(i):
            kp = (plane - back[0] - i // group) * group + lax.bitwise_xor(g, lax.rem(i, group))
            safe = jnp.maximum(kp, 0)
            active = (kp >= 0) & (kp <= qp) & (seg_ref[safe * n + n - 1] >= q_first)
            whole = (kp < qp) & (seg_ref[safe * n] == q_last)
            return kp, safe, active, whole

        def parts_of(i):
            return [s_s[i, :, t * HEAD : (t + 1) * HEAD] for t in range(lanes)]

        def score(i, carry):
            kp, safe, active, whole = state(i)

            @pl.when(active)
            def _():
                s_s[i] = lax.dot_general(
                    q_s[at], k_s[i], (((1,), (1,)), ((), ())), preferred_element_type=jnp.float32
                )

            @pl.when(active & whole)
            def _():
                m_s[...] = functools.reduce(jnp.maximum, parts_of(i), m_s[...])

            @pl.when(active & jnp.logical_not(whole))
            def _():
                seg_k = segrow_ref[pl.ds(safe, 1), :].astype(jnp.float32)
                ahead = lax.broadcasted_iota(jnp.int32, (n, HEAD), 1) - lax.broadcasted_iota(
                    jnp.int32, (n, HEAD), 0
                )
                for t in range(lanes):
                    lane = slice(t * HEAD, (t + 1) * HEAD)
                    seen = (ahead + t * HEAD <= (qp - kp) * n) & (seg_s[...] == seg_k[:, lane])
                    for h in range(heads):
                        row = slice(h * n, (h + 1) * n)
                        part = jnp.where(seen, s_s[i, row, lane], NEGATIVE)
                        s_s[i, row, lane] = part
                        m_s[row] = jnp.maximum(m_s[row], part)

            return carry

        def mix(i, carry):
            @pl.when(state(i)[2])
            def _():
                top = m_s[...]
                parts = [jnp.exp2((part - top) * scale) for part in parts_of(i)]
                l_s[...] += functools.reduce(jnp.add, parts)
                weights = jnp.concatenate([p.astype(jnp.bfloat16) for p in parts], axis=1)
                acc_s[...] += jnp.dot(weights, v_s[i], preferred_element_type=jnp.float32)

            return carry

        def both_passes():
            row = segrow_ref[pl.ds(qp, 1), :].astype(jnp.float32)
            seg_s[...] = jnp.broadcast_to(row, (HEAD, n)).T
            if carried:
                m_s[...] = given[0][...]
            else:
                m_s[...] = jnp.full(m_s.shape, NEGATIVE, jnp.float32)
            lax.fori_loop(0, n_kv, score, 0)
            top = jnp.broadcast_to(jnp.max(m_s[...], axis=1, keepdims=True), (rows, HEAD))
            if carried:
                shrink = jnp.exp2((given[0][...] - top) * scale)
                l_s[...] = given[1][...] * shrink
                acc_s[...] = given[2][...] * shrink
            else:
                l_s[...] = jnp.zeros(l_s.shape, jnp.float32)
                acc_s[...] = jnp.zeros(acc_s.shape, jnp.float32)
            m_s[...] = top
            lax.fori_loop(0, n_kv, mix, 0)

        def give(lane_sums, summed):
            for h in range(heads):
                row = slice(h * n, (h + 1) * n)
                total = jnp.sum(lane_sums[row], axis=1, keepdims=True)
                out_refs[0][at, :, h * HEAD : (h + 1) * HEAD] = (summed[row] / total).astype(jnp.bfloat16)

        if carried:
            needed = lax.fori_loop(
                0, n_kv, lambda i, seen: seen | state(i)[2].astype(jnp.int32), jnp.int32(0)
            )

            @pl.when(needed > 0)
            def _():
                both_passes()
                give(l_s[...], acc_s[...])

            @pl.when(needed == 0)
            def _():
                give(given[1][...], given[2][...])
        else:
            both_passes()
            if final:
                give(l_s[...], acc_s[...])
            else:
                for out_ref, value in zip(out_refs, (m_s, l_s, acc_s)):
                    out_ref[at] = value[...]
        return carry

    for pair in range(len(pairs)):
        lax.fori_loop(0, 2, functools.partial(one_query_piece, pair), 0)


def attention(group, heads, back, pairs, segments, q, kv, carried=None, final=True):
    n, width = q[0].shape[1:]
    rows, n_kv, n_q = heads * n, 2 * len(kv), 2 * len(pairs)
    state = jax.ShapeDtypeStruct((n_q, rows, HEAD), jnp.float32)
    if final:
        out_shape = [jax.ShapeDtypeStruct((n_q, n, width), jnp.bfloat16)]
    else:
        out_shape = [state] * 3
    carried = list(carried or ())
    found = pl.pallas_call(
        functools.partial(attention_kernel, group, heads, back, pairs, bool(carried), final),
        out_shape=out_shape,
        in_specs=[SMEM, VMEM] + [ANY] * (len(q) + len(kv)) + [VMEM] * len(carried),
        out_specs=[VMEM] * len(out_shape),
        scratch_shapes=[
            pltpu.VMEM((n_q, rows, HEAD), jnp.bfloat16),
            pltpu.VMEM((n_kv, n, HEAD), jnp.bfloat16),
            pltpu.VMEM((n_kv, n, HEAD), jnp.bfloat16),
            pltpu.VMEM((n_kv, rows, n), jnp.float32),
            pltpu.VMEM((rows, HEAD), jnp.float32),
            pltpu.VMEM((rows, HEAD), jnp.float32),
            pltpu.VMEM((rows, HEAD), jnp.float32),
            pltpu.VMEM((n, HEAD), jnp.float32),
            pltpu.SemaphoreType.DMA((n_q * heads + 2 * n_kv,)),
        ],
        compiler_params=params(28),
        cost_estimate=LIGHT,
        name="attention",
    )(segments, segments.reshape(-1, n), *q, *kv, *carried)
    return found[0] if final else found


def project_kernel(group, attn, planes, *refs):
    refs = list(refs)
    take = lambda count: [refs.pop(0) for _ in range(count)]
    w_refs, a_refs, out_refs = take(planes), take(group * attn), take(group * attn)
    a_s, w_s, a_sem, w_sem = refs
    z, _, y = place_in(group)
    n, width = a_refs[0].shape[1:]
    cols = w_refs[0].shape[1]
    rounds = planes // attn
    aligned = cols % HEAD == 0

    def a_copies(k):
        return [
            pltpu.make_async_copy(
                a_refs[i].at[(i % group) ^ k], a_s.at[k, :, pl.ds(i * width, width)], a_sem.at[k]
            )
            for i in range(attn * group)
        ]

    w_copies = []
    for turn in range(attn):
        to = xor(turn_of(z, y, planes, attn), turn)
        for r in range(rounds):
            place = to * rounds + r
            into = w_s.at[:, pl.ds(pl.multiple_of(place * cols, cols), cols)] if aligned else w_s.at[place]
            w_copies.append(pltpu.make_async_copy(w_refs[r + turn * rounds], into, w_sem))

    for copy in a_copies(0) + w_copies:
        copy.start()
    for k in range(1, group):
        for copy in a_copies(k):
            copy.start()
    for copy in w_copies:
        copy.wait()
    for k in range(group):
        for copy in a_copies(k):
            copy.wait()
        if aligned:
            found = jnp.dot(a_s[k], w_s[...], preferred_element_type=jnp.float32).astype(jnp.bfloat16)
            for to in range(attn):
                out_refs[to * group + k][...] = found[:, to * rounds * cols : (to + 1) * rounds * cols]
        else:
            for to in range(attn):
                for r in range(rounds):
                    out_refs[to * group + k][:, r * cols : (r + 1) * cols] = jnp.dot(
                        a_s[k], w_s[to * rounds + r], preferred_element_type=jnp.float32
                    ).astype(jnp.bfloat16)


def column_of(group, attn, planes, r, m, k, cols):
    z, g, y = place_in(group)
    rounds = planes // attn
    return ((xor(lax.rem(z, jnp.int32(rounds)), r) * group + xor(g, k)) * attn + xor(y, m)) * cols


def place_kernel(group, attn, planes, *refs):
    out_ref = refs[-1]
    rounds = planes // attn
    cols = refs[0].shape[1] // rounds
    for r in range(rounds):
        for m in range(attn):
            for k in range(group):
                at = pl.multiple_of(column_of(group, attn, planes, r, m, k, cols), cols)
                out_ref[:, pl.ds(at, cols)] = refs[m * group + k][:, r * cols : (r + 1) * cols]


def shards(dense, attn, queries, keys, values, segments, out_weight):
    n = queries.shape[0]
    tokens = segments.shape[0]
    group = keys.shape[1] // HEAD
    heads = queries.shape[1] // HEAD // group
    width = heads * HEAD
    planes = dense // group
    rounds = planes // attn
    hops = min(-(-(tokens // 2 - 1) // (n * group)), planes - 1)
    cols = out_weight.shape[1] // attn
    bf16 = lambda *shape: jax.ShapeDtypeStruct(shape, jnp.bfloat16)

    def number(z, g, y):
        return (z * group + g) * attn + y

    def pairs(move):
        found = []
        for z in range(planes):
            for g in range(group):
                for y in range(attn):
                    to = move(z, g, y)
                    if 0 <= to[0] < planes:
                        found.append((number(z, g, y), number(*to)))
        return found

    def across(array, j, m):
        with jax.named_scope(f"across_{j}_{m}"):
            return lax.ppermute(array, AXES, pairs(lambda z, g, y: (z, g ^ j, y ^ m)))

    def up(array, j=0):
        with jax.named_scope(f"up_{j}"):
            return lax.ppermute(array, AXES, pairs(lambda z, g, y: (z + 1, g ^ j, y)))

    def between(array, i):
        with jax.named_scope(f"between_{i}"):
            return lax.ppermute(array, AXES, pairs(lambda z, g, y: (z ^ i, g, y)))

    def with_other_core(arrays):
        return [which for array in arrays for which in (array, across(array, 1, 0))]

    after = lambda array, *others: lax.optimization_barrier((array, *others))

    pair = [bf16(2, n, 2 * HEAD)] * (group // 2)
    kv = pl.pallas_call(
        functools.partial(split_kv_kernel, group),
        out_shape=pair,
        in_specs=[VMEM] * 4,
        out_specs=[VMEM] * (group // 2),
        name="split_kv",
    )(keys, values, across(keys, 1, 0), across(values, 1, 0))
    links = [[kv[0]] + [across(kv[o], 2 * o, 0) for o in range(1, group // 2)]]
    links.append([up(kv[o], 2 * o) for o in range(group // 2)])

    queries, _ = after(queries, kv[0])
    q = pl.pallas_call(
        functools.partial(split_q_kernel, group),
        out_shape=[bf16(2, n, width)] * (group // 2),
        in_specs=[VMEM] * 2,
        out_specs=[VMEM] * (group // 2),
        name="split_q",
    )(queries, across(queries, 1, 0))
    out_weight, _ = after(out_weight, q[0])
    q = [q[0]] + [across(q[o], 2 * o, 0) for o in range(1, group // 2)]

    if cols % HEAD == 0:
        own = pl.pallas_call(
            functools.partial(split_w_kernel, group),
            out_shape=[bf16(out_weight.shape[0], cols)] * attn,
            in_specs=[VMEM],
            out_specs=[VMEM] * attn,
            name="split_w",
        )(out_weight)
    else:
        _, g, y = place_in(group)
        ordered = jnp.concatenate(
            [lax.dynamic_slice_in_dim(out_weight, xor(g, j) * width, width, 0) for j in range(group)]
        )
        own = [lax.dynamic_slice_in_dim(ordered, xor(y, m) * cols, cols, 1) for m in range(attn)]
    own = jnp.concatenate([own[0]] + [across(own[m], 0, m) for m in range(1, attn)])
    own, *links[1] = after(own, *links[1])
    for _ in range(1, hops):
        links.append([up(pair) for pair in links[-1]])
    blocks = {0: own}
    stride = planes // 2
    while stride:
        for i in list(blocks):
            blocks[i + stride] = between(blocks[i], stride)
        if stride == planes // 2:
            blocks[0], *links[-1] = after(own, *links[-1])
        stride //= 2

    near = [pair for pairs_of in links[:hops] for pair in pairs_of]
    carried = []
    for o in range(group // 2):
        carried += attention(group, heads, range(hops), [o], segments, [q[o]], near, final=False)
    attended = attention(
        group, heads, range(hops, hops + 1), range(group // 2), segments, q, links[hops], carried
    )

    everything = []
    for m in range(attn):
        everything += with_other_core(
            [attended if o == m == 0 else across(attended, 2 * o, m) for o in range(group // 2)]
        )

    w_shape = (attn * group * width, planes * cols) if cols % HEAD == 0 else (planes, attn * group * width, cols)
    found = pl.pallas_call(
        functools.partial(project_kernel, group, attn, planes),
        out_shape=[bf16(n, rounds * cols)] * (attn * group),
        in_specs=[ANY] * (planes + group * attn),
        out_specs=[VMEM] * (attn * group),
        scratch_shapes=[
            pltpu.VMEM((group, n, attn * group * width), jnp.bfloat16),
            pltpu.VMEM(w_shape, jnp.bfloat16),
            pltpu.SemaphoreType.DMA((group,)),
            pltpu.SemaphoreType.DMA,
        ],
        compiler_params=params(28),
        cost_estimate=LIGHT,
        name="project",
    )(*[blocks[i] for i in range(planes)], *everything)
    placed = []
    for m in range(attn):
        for k in range(group):
            piece = found[m * group + k]
            placed.append(piece if m == k == 0 else across(piece, k, m))

    if cols % HEAD == 0:
        return pl.pallas_call(
            functools.partial(place_kernel, group, attn, planes),
            out_shape=bf16(n, planes * group * cols),
            in_specs=[VMEM] * len(placed),
            out_specs=VMEM,
            name="place",
        )(*placed)
    out = jnp.zeros((n, planes * group * cols), jnp.bfloat16)
    for r in range(rounds):
        for m in range(attn):
            for k in range(group):
                part = placed[m * group + k][:, r * cols : (r + 1) * cols]
                at = column_of(group, attn, planes, r, m, k, cols)
                out = lax.dynamic_update_slice_in_dim(out, part, at, 1)
    return out


def solution(mesh):
    return jax.shard_map(
        functools.partial(shards, mesh.shape["dense"], mesh.shape["attn"]),
        mesh=mesh,
        in_specs=(
            P("dense", "attn"),
            P("dense", "attn"),
            P("dense", "attn"),
            P(),
            P("attn", "dense"),
        ),
        out_specs=P("dense", "attn"),
        check_vma=False,
    )
```

```python
import functools
import math

import jax
import jax.numpy as jnp
from jax import lax
from jax.experimental import pallas as pl
from jax.experimental.pallas import tpu as pltpu
from jax.sharding import PartitionSpec as P

HEAD = 128
NEGATIVE = -1e30
AXES = ("dense", "attn")
ANY = pl.BlockSpec(memory_space=pl.ANY)
SMEM = pl.BlockSpec(memory_space=pltpu.SMEM)
VMEM = pl.BlockSpec(memory_space=pltpu.VMEM)
LIGHT = pl.CostEstimate(flops=0, bytes_accessed=0, transcendentals=0)


def xor(a, b):
    return lax.bitwise_xor(a, jnp.int32(b))


def params(mib):
    return pltpu.CompilerParams(vmem_limit_bytes=mib * 2**20)


def place_in(group):
    device = lax.axis_index("dense").astype(jnp.int32)
    return device // group, lax.rem(device, jnp.int32(group)), lax.axis_index("attn").astype(jnp.int32)


def turn_of(z, y, planes, attn):
    return lax.bitwise_xor(z // (planes // attn), y)


def split_qkv_kernel(group, *refs):
    g = place_in(group)[1]
    kv_outs, q_outs = refs[6 : 6 + group // 2], refs[6 + group // 2 :]
    width = q_outs[0].shape[2]
    for core in range(2):
        k_ref, v_ref, q_ref = refs[3 * core : 3 * core + 3]
        for o in range(group // 2):
            at = pl.ds(pl.multiple_of(xor(g, 2 * o) * HEAD, HEAD), HEAD)
            kv_outs[o][core, :, :HEAD] = k_ref[:, at]
            kv_outs[o][core, :, HEAD:] = v_ref[:, at]
            q_outs[o][core] = q_ref[:, pl.ds(pl.multiple_of(xor(g, 2 * o) * width, width), width)]


def split_w_kernel(group, w_ref, *outs):
    g, y = place_in(group)[1:]
    rows, cols = outs[0].shape
    width = rows // group
    for m, out in enumerate(outs):
        at = pl.ds(pl.multiple_of(xor(y, m) * cols, cols), cols)
        for j in range(group):
            part = w_ref[pl.ds(pl.multiple_of(xor(g, j) * width, width), width), at]
            out[j * width : (j + 1) * width, :] = part


def attention_kernel(group, heads, back, pairs, carried, final, seg_ref, segrow_ref, *refs):
    n_kv, n_q = len(back) * group, len(pairs) * 2
    refs = list(refs)
    take = lambda count: [refs.pop(0) for _ in range(count)]
    q_refs, kv_refs = take(len(pairs)), take(n_kv // 2)
    state_refs = [take(2) for _ in pairs] if carried else None
    out_refs = take(1 if final else 2)
    q_s, k_s, v_s, m_own, acc_own, seg_s, sem = refs
    n = segrow_ref.shape[1]
    rows = heads * n
    lanes = n // HEAD
    copies = []
    for k in range(n_q):
        for h in range(heads):
            q_part = q_refs[k // 2].at[k % 2, :, pl.ds(h * HEAD, HEAD)]
            copies.append((q_part, q_s.at[k, pl.ds(h * n, n), :]))
    for i in range(n_kv):
        kv = kv_refs[i // 2].at[i % 2]
        at = pl.ds(i % 2 * n, n)
        copies.append((kv.at[:, pl.ds(0, HEAD)], k_s.at[i // 2, at, :]))
        copies.append((kv.at[:, pl.ds(HEAD, HEAD)], v_s.at[i // 2, at, pl.ds(0, HEAD)]))
    copies = [pltpu.make_async_copy(a, b, sem.at[i]) for i, (a, b) in enumerate(copies)]
    for c in copies:
        c.start()
    v_s[:, :, HEAD:] = jnp.ones((n_kv // 2, 2 * n, HEAD), jnp.bfloat16)
    for c in copies:
        c.wait()

    plane, g, _ = place_in(group)
    scale = math.log2(math.e) / math.sqrt(HEAD)

    def one_query_piece(pair, core, carry):
        at = 2 * pair + core
        given = [ref.at[core] for ref in state_refs[pair]] if carried else None
        m_s, acc_s = (m_own, acc_own) if final else (ref.at[at] for ref in out_refs)
        qp = plane * group + lax.bitwise_xor(g, 2 * pairs[pair] + core)
        q_first, q_last = seg_ref[qp * n], seg_ref[qp * n + n - 1]

        def piece(i, which):
            place = lax.bitwise_xor(g, 2 * lax.rem(i, group // 2) + which)
            kp = (plane - back[0] - i // (group // 2)) * group + place
            safe = jnp.maximum(kp, 0)
            active = (kp >= 0) & (kp <= qp) & (seg_ref[safe * n + n - 1] >= q_first)
            whole = (kp >= 0) & (kp < qp) & (seg_ref[safe * n] == q_last)
            return kp, safe, active, whole

        def needed(i):
            return piece(i, 0)[2] | piece(i, 1)[2]

        def mix(i, carry):
            pieces = [piece(i, which) for which in range(2)]
            active = pieces[0][2] | pieces[1][2]
            whole = pieces[0][3] & pieces[1][3]

            def scores(h):
                return lax.dot_general(
                    q_s[at, h * n : (h + 1) * n],
                    k_s[i],
                    (((1,), (1,)), ((), ())),
                    preferred_element_type=jnp.float32,
                )

            def each_head(seen):
                ahead = scores(0)
                for h in range(heads):
                    s, ahead = ahead, scores(h + 1) if h + 1 < heads else None
                    head(h, s, seen)

            def head(h, s, seen):
                row = slice(h * n, (h + 1) * n)
                if seen is not None:
                    s = jnp.where(seen, s, NEGATIVE)
                old = m_s[row]
                top = jnp.maximum(old, jnp.max(s, axis=1, keepdims=True))
                m_s[row] = top
                shrink = jnp.exp2((old - top) * scale)
                top = jnp.concatenate([top] * (2 * lanes), axis=1)
                weights = jnp.exp2((s - top) * scale).astype(jnp.bfloat16)
                found = jnp.dot(weights, v_s[i], preferred_element_type=jnp.float32)
                acc_s[row] = acc_s[row] * jnp.concatenate([shrink] * 2, axis=1) + found

            @pl.when(active & whole)
            def _():
                each_head(None)

            @pl.when(active & jnp.logical_not(whole))
            def _():
                ahead = lax.broadcasted_iota(jnp.int32, (n, HEAD), 1) - lax.broadcasted_iota(
                    jnp.int32, (n, HEAD), 0
                )
                seen = []
                for kp, safe, _, _ in pieces:
                    seg_k = segrow_ref[pl.ds(safe, 1), :].astype(jnp.float32)
                    for t in range(lanes):
                        same = seg_s[...] == seg_k[:, t * HEAD : (t + 1) * HEAD]
                        seen.append(same & (ahead + t * HEAD <= (qp - kp) * n) & (kp >= 0))
                seen = jnp.concatenate(seen, axis=1)
                each_head(seen)

            return carry

        def give(summed):
            for h in range(heads):
                row = slice(h * n, (h + 1) * n)
                out_refs[0][at, :, h * HEAD : (h + 1) * HEAD] = (
                    summed[row, :HEAD] / summed[row, HEAD:]
                ).astype(jnp.bfloat16)

        def all_keys():
            seg_row = segrow_ref[pl.ds(qp, 1), :].astype(jnp.float32)
            seg_s[...] = jnp.broadcast_to(seg_row, (HEAD, n)).T
            if carried:
                m_s[...] = given[0][...]
                acc_s[...] = given[1][...]
            else:
                m_s[...] = jnp.full(m_s.shape, NEGATIVE, jnp.float32)
                acc_s[...] = jnp.zeros(acc_s.shape, jnp.float32)
            lax.fori_loop(0, n_kv // 2, mix, 0)

        if carried:
            any_needed = lax.fori_loop(
                0, n_kv // 2, lambda i, seen: seen | needed(i).astype(jnp.int32), jnp.int32(0)
            )

            @pl.when(any_needed > 0)
            def _():
                all_keys()
                give(acc_s)

            @pl.when(any_needed == 0)
            def _():
                give(given[1])
        else:
            all_keys()
            if final:
                give(acc_s)
        return carry

    for pair in range(len(pairs)):
        lax.fori_loop(0, 2, functools.partial(one_query_piece, pair), 0)


def attention(group, heads, back, pairs, segments, q, kv, carried=None, final=True):
    n, width = q[0].shape[1:]
    rows, n_kv, n_q = heads * n, 2 * len(kv), 2 * len(pairs)
    if final:
        out_shape = [jax.ShapeDtypeStruct((n_q, n, width), jnp.bfloat16)]
    else:
        out_shape = [jax.ShapeDtypeStruct((n_q, rows, lanes), jnp.float32) for lanes in (HEAD, 2 * HEAD)]
    carried = list(carried or ())
    found = pl.pallas_call(
        functools.partial(attention_kernel, group, heads, back, pairs, bool(carried), final),
        out_shape=out_shape,
        in_specs=[SMEM, VMEM] + [ANY] * (len(q) + len(kv)) + [VMEM] * len(carried),
        out_specs=[VMEM] * len(out_shape),
        scratch_shapes=[
            pltpu.VMEM((n_q, rows, HEAD), jnp.bfloat16),
            pltpu.VMEM((n_kv // 2, 2 * n, HEAD), jnp.bfloat16),
            pltpu.VMEM((n_kv // 2, 2 * n, 2 * HEAD), jnp.bfloat16),
            pltpu.VMEM((rows, HEAD), jnp.float32),
            pltpu.VMEM((rows, 2 * HEAD), jnp.float32),
            pltpu.VMEM((n, HEAD), jnp.float32),
            pltpu.SemaphoreType.DMA((n_q * heads + 2 * n_kv,)),
        ],
        compiler_params=params(28),
        cost_estimate=LIGHT,
        name="attention",
    )(segments, segments.reshape(-1, n), *q, *kv, *carried)
    return found[0] if final else found


def project_kernel(group, attn, planes, *refs):
    refs = list(refs)
    take = lambda count: [refs.pop(0) for _ in range(count)]
    w_refs, a_refs, out_refs = take(planes), take(group * attn), take(group * attn)
    a_s, w_s, a_sem, w_sem = refs
    z, _, y = place_in(group)
    n, width = a_refs[0].shape[1:]
    cols = w_refs[0].shape[1]
    rounds = planes // attn
    aligned = cols % HEAD == 0

    def a_copies(k):
        return [
            pltpu.make_async_copy(
                a_refs[i].at[(i % group) ^ k], a_s.at[k, :, pl.ds(i * width, width)], a_sem.at[k]
            )
            for i in range(attn * group)
        ]

    w_copies = []
    for turn in range(attn):
        to = xor(turn_of(z, y, planes, attn), turn)
        for r in range(rounds):
            place = to * rounds + r
            into = w_s.at[:, pl.ds(pl.multiple_of(place * cols, cols), cols)] if aligned else w_s.at[place]
            w_copies.append(pltpu.make_async_copy(w_refs[r + turn * rounds], into, w_sem))

    for copy in a_copies(0) + w_copies:
        copy.start()
    for k in range(1, group):
        for copy in a_copies(k):
            copy.start()
    for copy in w_copies:
        copy.wait()
    for k in range(group):
        for copy in a_copies(k):
            copy.wait()
        if aligned:
            found = jnp.dot(a_s[k], w_s[...], preferred_element_type=jnp.float32).astype(jnp.bfloat16)
            for to in range(attn):
                out_refs[to * group + k][...] = found[:, to * rounds * cols : (to + 1) * rounds * cols]
        else:
            for to in range(attn):
                for r in range(rounds):
                    out_refs[to * group + k][:, r * cols : (r + 1) * cols] = jnp.dot(
                        a_s[k], w_s[to * rounds + r], preferred_element_type=jnp.float32
                    ).astype(jnp.bfloat16)


def column_of(group, attn, planes, r, m, k, cols):
    z, g, y = place_in(group)
    rounds = planes // attn
    return ((xor(lax.rem(z, jnp.int32(rounds)), r) * group + xor(g, k)) * attn + xor(y, m)) * cols


def place_kernel(group, attn, planes, *refs):
    out_ref = refs[-1]
    rounds = planes // attn
    cols = refs[0].shape[1] // rounds
    for r in range(rounds):
        for m in range(attn):
            for k in range(group):
                at = pl.multiple_of(column_of(group, attn, planes, r, m, k, cols), cols)
                out_ref[:, pl.ds(at, cols)] = refs[m * group + k][:, r * cols : (r + 1) * cols]


def shards(dense, attn, queries, keys, values, segments, out_weight):
    n = queries.shape[0]
    tokens = segments.shape[0]
    group = keys.shape[1] // HEAD
    heads = queries.shape[1] // HEAD // group
    width = heads * HEAD
    planes = dense // group
    rounds = planes // attn
    hops = min(-(-(tokens // 2 - 1) // (n * group)), planes - 1)
    cols = out_weight.shape[1] // attn
    bf16 = lambda *shape: jax.ShapeDtypeStruct(shape, jnp.bfloat16)

    def number(z, g, y):
        return (z * group + g) * attn + y

    def pairs(move):
        found = []
        for z in range(planes):
            for g in range(group):
                for y in range(attn):
                    to = move(z, g, y)
                    if 0 <= to[0] < planes:
                        found.append((number(z, g, y), number(*to)))
        return found

    def across(array, j, m):
        with jax.named_scope(f"across_{j}_{m}"):
            return lax.ppermute(array, AXES, pairs(lambda z, g, y: (z, g ^ j, y ^ m)))

    def up(array, j=0):
        with jax.named_scope(f"up_{j}"):
            return lax.ppermute(array, AXES, pairs(lambda z, g, y: (z + 1, g ^ j, y)))

    def between(array, i):
        with jax.named_scope(f"between_{i}"):
            return lax.ppermute(array, AXES, pairs(lambda z, g, y: (z ^ i, g, y)))

    def with_other_core(arrays):
        return [which for array in arrays for which in (array, across(array, 1, 0))]

    after = lambda array, *others: lax.optimization_barrier((array, *others))

    if cols % HEAD == 0:
        own = pl.pallas_call(
            functools.partial(split_w_kernel, group),
            out_shape=[bf16(out_weight.shape[0], cols)] * attn,
            in_specs=[VMEM],
            out_specs=[VMEM] * attn,
            name="split_w",
        )(out_weight)
    else:
        _, g, y = place_in(group)
        ordered = jnp.concatenate(
            [lax.dynamic_slice_in_dim(out_weight, xor(g, j) * width, width, 0) for j in range(group)]
        )
        own = [lax.dynamic_slice_in_dim(ordered, xor(y, m) * cols, cols, 1) for m in range(attn)]
    others = [own[0]] + [across(own[m], 0, m) for m in range(1, attn)]

    keys, *own = after(keys, *own)
    near = [keys, values, queries]
    split = pl.pallas_call(
        functools.partial(split_qkv_kernel, group),
        out_shape=[bf16(2, n, 2 * HEAD)] * (group // 2) + [bf16(2, n, width)] * (group // 2),
        in_specs=[VMEM] * 6,
        out_specs=[VMEM] * group,
        name="split_qkv",
    )(*near, *[across(array, 1, 0) for array in near])
    kv, q = split[: group // 2], split[group // 2 :]
    links = [[kv[0]] + [across(kv[o], 2 * o, 0) for o in range(1, group // 2)]]
    links.append([up(kv[o], 2 * o) for o in range(group // 2)])
    q = [q[0]] + [across(q[o], 2 * o, 0) for o in range(1, group // 2)]

    own = jnp.concatenate(others)
    own, *links[1] = after(own, *links[1])
    for _ in range(1, hops):
        links.append([up(pair) for pair in links[-1]])
    blocks = {0: own}
    stride = planes // 2
    while stride:
        for i in list(blocks):
            blocks[i + stride] = between(blocks[i], stride)
        stride //= 2

    near = [pair for pairs_of in links[:hops] for pair in pairs_of]
    carried = []
    for o in range(group // 2):
        carried += attention(group, heads, range(hops), [o], segments, [q[o]], near, final=False)
    attended = attention(
        group, heads, range(hops, hops + 1), range(group // 2), segments, q, links[hops], carried
    )

    everything = []
    for m in range(attn):
        everything += with_other_core(
            [attended if o == m == 0 else across(attended, 2 * o, m) for o in range(group // 2)]
        )

    w_shape = (attn * group * width, planes * cols) if cols % HEAD == 0 else (planes, attn * group * width, cols)
    found = pl.pallas_call(
        functools.partial(project_kernel, group, attn, planes),
        out_shape=[bf16(n, rounds * cols)] * (attn * group),
        in_specs=[ANY] * (planes + group * attn),
        out_specs=[VMEM] * (attn * group),
        scratch_shapes=[
            pltpu.VMEM((group, n, attn * group * width), jnp.bfloat16),
            pltpu.VMEM(w_shape, jnp.bfloat16),
            pltpu.SemaphoreType.DMA((group,)),
            pltpu.SemaphoreType.DMA,
        ],
        compiler_params=params(28),
        cost_estimate=LIGHT,
        name="project",
    )(*[blocks[i] for i in range(planes)], *everything)
    placed = []
    for m in range(attn):
        for k in range(group):
            piece = found[m * group + k]
            placed.append(piece if m == k == 0 else across(piece, k, m))

    if cols % HEAD == 0:
        return pl.pallas_call(
            functools.partial(place_kernel, group, attn, planes),
            out_shape=bf16(n, planes * group * cols),
            in_specs=[VMEM] * len(placed),
            out_specs=VMEM,
            name="place",
        )(*placed)
    out = jnp.zeros((n, planes * group * cols), jnp.bfloat16)
    for r in range(rounds):
        for m in range(attn):
            for k in range(group):
                part = placed[m * group + k][:, r * cols : (r + 1) * cols]
                at = column_of(group, attn, planes, r, m, k, cols)
                out = lax.dynamic_update_slice_in_dim(out, part, at, 1)
    return out


def solution(mesh):
    return jax.shard_map(
        functools.partial(shards, mesh.shape["dense"], mesh.shape["attn"]),
        mesh=mesh,
        in_specs=(
            P("dense", "attn"),
            P("dense", "attn"),
            P("dense", "attn"),
            P(),
            P("attn", "dense"),
        ),
        out_specs=P("dense", "attn"),
        check_vma=False,
    )
```

```python
import functools
import math

import jax
import jax.numpy as jnp
from jax import lax
from jax.experimental import pallas as pl
from jax.experimental.pallas import tpu as pltpu
from jax.sharding import PartitionSpec as P

HEAD = 128
NEGATIVE = -1e30
AXES = ("dense", "attn")
ANY = pl.BlockSpec(memory_space=pl.ANY)
SMEM = pl.BlockSpec(memory_space=pltpu.SMEM)
VMEM = pl.BlockSpec(memory_space=pltpu.VMEM)
LIGHT = pl.CostEstimate(flops=0, bytes_accessed=0, transcendentals=0)


def xor(a, b):
    return lax.bitwise_xor(a, jnp.int32(b))


def params(mib):
    return pltpu.CompilerParams(vmem_limit_bytes=mib * 2**20)


def place_in(group):
    device = lax.axis_index("dense").astype(jnp.int32)
    return device // group, lax.rem(device, jnp.int32(group)), lax.axis_index("attn").astype(jnp.int32)


def turn_of(z, y, planes, attn):
    return lax.bitwise_xor(z // (planes // attn), y)


def split_kv_kernel(group, *refs):
    g = place_in(group)[1]
    for core in range(2):
        k_ref, v_ref = refs[2 * core : 2 * core + 2]
        for o, out in enumerate(refs[4:]):
            at = pl.ds(pl.multiple_of(xor(g, 2 * o) * HEAD, HEAD), HEAD)
            out[core, :, :HEAD] = k_ref[:, at]
            out[core, :, HEAD:] = v_ref[:, at]


def split_q_kernel(group, *refs):
    g = place_in(group)[1]
    width = refs[2].shape[2]
    for core in range(2):
        for o, out in enumerate(refs[2:]):
            out[core] = refs[core][:, pl.ds(pl.multiple_of(xor(g, 2 * o) * width, width), width)]


def split_w_kernel(group, w_ref, *outs):
    g, y = place_in(group)[1:]
    rows, cols = outs[0].shape
    width = rows // group
    for m, out in enumerate(outs):
        at = pl.ds(pl.multiple_of(xor(y, m) * cols, cols), cols)
        for j in range(group):
            part = w_ref[pl.ds(pl.multiple_of(xor(g, j) * width, width), width), at]
            out[j * width : (j + 1) * width, :] = part


def attention_kernel(group, heads, back, pairs, carried, final, seg_ref, segrow_ref, *refs):
    n_kv, n_q = len(back) * group, len(pairs) * 2
    refs = list(refs)
    take = lambda count: [refs.pop(0) for _ in range(count)]
    q_refs, kv_refs = take(len(pairs)), take(n_kv // 2)
    state_refs = [take(2) for _ in pairs] if carried else None
    out_refs = take(1 if final else 2)
    q_s, k_s, v_s, m_own, acc_own, seg_s, sem = refs
    unit = k_s.shape[1] // segrow_ref.shape[1]
    n = segrow_ref.shape[1]
    rows = heads * n
    lanes = n // HEAD
    copies = []
    for k in range(n_q):
        for h in range(heads):
            q_part = q_refs[k // 2].at[k % 2, :, pl.ds(h * HEAD, HEAD)]
            copies.append((q_part, q_s.at[k, pl.ds(h * n, n), :]))
    for i in range(n_kv):
        kv = kv_refs[i // 2].at[i % 2]
        at = pl.ds(i % unit * n, n)
        copies.append((kv.at[:, pl.ds(0, HEAD)], k_s.at[i // unit, at, :]))
        copies.append((kv.at[:, pl.ds(HEAD, HEAD)], v_s.at[i // unit, at, pl.ds(0, HEAD)]))
    copies = [pltpu.make_async_copy(a, b, sem.at[i]) for i, (a, b) in enumerate(copies)]
    for c in copies:
        c.start()
    v_s[:, :, HEAD:] = jnp.ones((n_kv // unit, unit * n, HEAD), jnp.bfloat16)
    for c in copies:
        c.wait()

    plane, g, _ = place_in(group)
    scale = math.log2(math.e) / math.sqrt(HEAD)

    def one_query_piece(pair, core, carry):
        at = 2 * pair + core
        given = [ref.at[core] for ref in state_refs[pair]] if carried else None
        m_s, acc_s = (m_own, acc_own) if final else (ref.at[at] for ref in out_refs)
        qp = plane * group + lax.bitwise_xor(g, 2 * pairs[pair] + core)
        q_first, q_last = seg_ref[qp * n], seg_ref[qp * n + n - 1]

        def piece(i, which):
            i = i * unit + which
            kp = (plane - back[0] - i // group) * group + lax.bitwise_xor(g, lax.rem(i, group))
            safe = jnp.maximum(kp, 0)
            active = (kp >= 0) & (kp <= qp) & (seg_ref[safe * n + n - 1] >= q_first)
            whole = (kp >= 0) & (kp < qp) & (seg_ref[safe * n] == q_last)
            return kp, safe, active, whole

        def needed(i):
            return functools.reduce(jnp.logical_or, [piece(i, which)[2] for which in range(unit)])

        def mix(i, carry):
            pieces = [piece(i, which) for which in range(unit)]
            active = needed(i)
            whole = functools.reduce(jnp.logical_and, [p[3] for p in pieces])

            def scores(h):
                return lax.dot_general(
                    q_s[at, h * n : (h + 1) * n],
                    k_s[i],
                    (((1,), (1,)), ((), ())),
                    preferred_element_type=jnp.float32,
                )

            def each_head(seen):
                ahead = scores(0)
                for h in range(heads):
                    s, ahead = ahead, scores(h + 1) if h + 1 < heads else None
                    head(h, s, seen)

            def head(h, s, seen):
                row = slice(h * n, (h + 1) * n)
                if seen is not None:
                    s = jnp.where(seen, s, NEGATIVE)
                old = m_s[row]
                top = jnp.maximum(old, jnp.max(s, axis=1, keepdims=True))
                m_s[row] = top
                shrink = jnp.exp2((old - top) * scale)
                top = jnp.concatenate([top] * (unit * lanes), axis=1)
                weights = jnp.exp2((s - top) * scale).astype(jnp.bfloat16)
                found = jnp.dot(weights, v_s[i], preferred_element_type=jnp.float32)
                acc_s[row] = acc_s[row] * jnp.concatenate([shrink] * 2, axis=1) + found

            @pl.when(active & whole)
            def _():
                each_head(None)

            @pl.when(active & jnp.logical_not(whole))
            def _():
                ahead = lax.broadcasted_iota(jnp.int32, (n, HEAD), 1) - lax.broadcasted_iota(
                    jnp.int32, (n, HEAD), 0
                )
                seen = []
                for kp, safe, _, _ in pieces:
                    seg_k = segrow_ref[pl.ds(safe, 1), :].astype(jnp.float32)
                    for t in range(lanes):
                        same = seg_s[...] == seg_k[:, t * HEAD : (t + 1) * HEAD]
                        seen.append(same & (ahead + t * HEAD <= (qp - kp) * n) & (kp >= 0))
                seen = jnp.concatenate(seen, axis=1)
                each_head(seen)

            return carry

        def give(summed):
            for h in range(heads):
                row = slice(h * n, (h + 1) * n)
                out_refs[0][at, :, h * HEAD : (h + 1) * HEAD] = (
                    summed[row, :HEAD] / summed[row, HEAD:]
                ).astype(jnp.bfloat16)

        def all_keys():
            seg_row = segrow_ref[pl.ds(qp, 1), :].astype(jnp.float32)
            seg_s[...] = jnp.broadcast_to(seg_row, (HEAD, n)).T
            if carried:
                m_s[...] = given[0][...]
                acc_s[...] = given[1][...]
            else:
                m_s[...] = jnp.full(m_s.shape, NEGATIVE, jnp.float32)
                acc_s[...] = jnp.zeros(acc_s.shape, jnp.float32)
            lax.fori_loop(0, n_kv // unit, mix, 0)

        if carried:
            any_needed = lax.fori_loop(
                0, n_kv // unit, lambda i, seen: seen | needed(i).astype(jnp.int32), jnp.int32(0)
            )

            @pl.when(any_needed > 0)
            def _():
                all_keys()
                give(acc_s)

            @pl.when(any_needed == 0)
            def _():
                give(given[1])
        else:
            all_keys()
            if final:
                give(acc_s)
        return carry

    for pair in range(len(pairs)):
        lax.fori_loop(0, 2, functools.partial(one_query_piece, pair), 0)


def attention(group, heads, back, pairs, segments, q, kv, carried=None, final=True):
    n, width = q[0].shape[1:]
    rows, n_kv, n_q = heads * n, 2 * len(kv), 2 * len(pairs)
    if final:
        out_shape = [jax.ShapeDtypeStruct((n_q, n, width), jnp.bfloat16)]
    else:
        out_shape = [jax.ShapeDtypeStruct((n_q, rows, lanes), jnp.float32) for lanes in (HEAD, 2 * HEAD)]
    carried = list(carried or ())
    unit = 1 if carried else 2
    found = pl.pallas_call(
        functools.partial(attention_kernel, group, heads, back, pairs, bool(carried), final),
        out_shape=out_shape,
        in_specs=[SMEM, VMEM] + [ANY] * (len(q) + len(kv)) + [VMEM] * len(carried),
        out_specs=[VMEM] * len(out_shape),
        scratch_shapes=[
            pltpu.VMEM((n_q, rows, HEAD), jnp.bfloat16),
            pltpu.VMEM((n_kv // unit, unit * n, HEAD), jnp.bfloat16),
            pltpu.VMEM((n_kv // unit, unit * n, 2 * HEAD), jnp.bfloat16),
            pltpu.VMEM((rows, HEAD), jnp.float32),
            pltpu.VMEM((rows, 2 * HEAD), jnp.float32),
            pltpu.VMEM((n, HEAD), jnp.float32),
            pltpu.SemaphoreType.DMA((n_q * heads + 2 * n_kv,)),
        ],
        compiler_params=params(28),
        cost_estimate=LIGHT,
        name="attention",
    )(segments, segments.reshape(-1, n), *q, *kv, *carried)
    return found[0] if final else found


def project_kernel(group, attn, planes, *refs):
    refs = list(refs)
    take = lambda count: [refs.pop(0) for _ in range(count)]
    w_refs, a_refs, out_refs = take(planes), take(group * attn), take(group * attn)
    z, _, y = place_in(group)
    cols = w_refs[0].shape[1]
    rounds = planes // attn
    turn = turn_of(z, y, planes, attn)
    for k in range(group):
        rows = jnp.concatenate([a_refs[i][(i % group) ^ k] for i in range(attn * group)], axis=1)
        dot = lambda weights: jnp.dot(rows, weights, preferred_element_type=jnp.float32).astype(jnp.bfloat16)
        if cols % HEAD == 0:
            found = dot(jnp.concatenate([w_ref[...] for w_ref in w_refs], axis=1))
            found = [found[:, t * rounds * cols : (t + 1) * rounds * cols] for t in range(attn)]
        else:
            found = [
                jnp.concatenate([dot(w_ref[...]) for w_ref in w_refs[t * rounds : (t + 1) * rounds]], axis=1)
                for t in range(attn)
            ]
        for to in range(attn):
            here = xor(turn, to)
            mine = found[0]
            for t in range(1, attn):
                mine = jnp.where(here == t, found[t], mine)
            out_refs[to * group + k][...] = mine


def farthest_first(attn, group):
    return sorted(((m, k) for m in range(attn) for k in range(group)), key=lambda at: (at[1] > 1, at[0] > 0, at[1]))[
        ::-1
    ]


def column_of(group, attn, planes, r, m, k, cols):
    z, g, y = place_in(group)
    rounds = planes // attn
    return ((xor(lax.rem(z, jnp.int32(rounds)), r) * group + xor(g, k)) * attn + xor(y, m)) * cols


def place_kernel(group, attn, planes, *refs):
    out_ref = refs[-1]
    rounds = planes // attn
    cols = refs[0].shape[1] // rounds
    for r in range(rounds):
        for (m, k), ref in zip(farthest_first(attn, group), refs):
            at = pl.multiple_of(column_of(group, attn, planes, r, m, k, cols), cols)
            out_ref[:, pl.ds(at, cols)] = ref[:, r * cols : (r + 1) * cols]


def shards(dense, attn, queries, keys, values, segments, out_weight):
    n = queries.shape[0]
    tokens = segments.shape[0]
    group = keys.shape[1] // HEAD
    heads = queries.shape[1] // HEAD // group
    width = heads * HEAD
    planes = dense // group
    rounds = planes // attn
    hops = min(-(-(tokens // 2 - 1) // (n * group)), planes - 1)
    cols = out_weight.shape[1] // attn
    bf16 = lambda *shape: jax.ShapeDtypeStruct(shape, jnp.bfloat16)

    def number(z, g, y):
        return (z * group + g) * attn + y

    def pairs(move):
        found = []
        for z in range(planes):
            for g in range(group):
                for y in range(attn):
                    to = move(z, g, y)
                    if 0 <= to[0] < planes:
                        found.append((number(z, g, y), number(*to)))
        return found

    def across(array, j, m):
        with jax.named_scope(f"across_{j}_{m}"):
            return lax.ppermute(array, AXES, pairs(lambda z, g, y: (z, g ^ j, y ^ m)))

    def up(array, j=0):
        with jax.named_scope(f"up_{j}"):
            return lax.ppermute(array, AXES, pairs(lambda z, g, y: (z + 1, g ^ j, y)))

    def between(array, i):
        with jax.named_scope(f"between_{i}"):
            return lax.ppermute(array, AXES, pairs(lambda z, g, y: (z ^ i, g, y)))

    def with_other_core(arrays):
        return [which for array in arrays for which in (array, across(array, 1, 0))]

    after = lambda array, *others: lax.optimization_barrier((array, *others))

    if cols % HEAD == 0:
        own = pl.pallas_call(
            functools.partial(split_w_kernel, group),
            out_shape=[bf16(out_weight.shape[0], cols)] * attn,
            in_specs=[VMEM],
            out_specs=[VMEM] * attn,
            name="split_w",
        )(out_weight)
    else:
        _, g, y = place_in(group)
        ordered = jnp.concatenate(
            [lax.dynamic_slice_in_dim(out_weight, xor(g, j) * width, width, 0) for j in range(group)]
        )
        own = [lax.dynamic_slice_in_dim(ordered, xor(y, m) * cols, cols, 1) for m in range(attn)]
    others = [own[0]] + [across(own[m], 0, m) for m in range(1, attn)]

    keys, *own = after(keys, *own)
    kv = pl.pallas_call(
        functools.partial(split_kv_kernel, group),
        out_shape=[bf16(2, n, 2 * HEAD)] * (group // 2),
        in_specs=[VMEM] * 4,
        out_specs=[VMEM] * (group // 2),
        name="split_kv",
    )(keys, values, across(keys, 1, 0), across(values, 1, 0))
    links = [[kv[0]] + [across(kv[o], 2 * o, 0) for o in range(1, group // 2)]]
    links.append([up(kv[o], 2 * o) for o in range(group // 2)])

    queries, far_queries, *others = after(queries, across(queries, 1, 0), *others)
    q = pl.pallas_call(
        functools.partial(split_q_kernel, group),
        out_shape=[bf16(2, n, width)] * (group // 2),
        in_specs=[VMEM] * 2,
        out_specs=[VMEM] * (group // 2),
        name="split_q",
    )(queries, far_queries)
    q = [q[0]] + [across(q[o], 2 * o, 0) for o in range(1, group // 2)]

    own = jnp.concatenate(others)
    own, *links[1] = after(own, *links[1])
    for _ in range(1, hops):
        links.append([up(pair) for pair in links[-1]])
    blocks = {0: own}
    stride = planes // 2
    while stride:
        for i in list(blocks):
            blocks[i + stride] = between(blocks[i], stride)
        stride //= 2

    near = [pair for pairs_of in links[:hops] for pair in pairs_of]
    carried = []
    for o in range(group // 2):
        carried += attention(group, heads, range(hops), [o], segments, [q[o]], near, final=False)
    attended = attention(
        group, heads, range(hops, hops + 1), range(group // 2), segments, q, links[hops], carried
    )

    everything = []
    for m in range(attn):
        everything += with_other_core(
            [attended if o == m == 0 else across(attended, 2 * o, m) for o in range(group // 2)]
        )

    found = pl.pallas_call(
        functools.partial(project_kernel, group, attn, planes),
        out_shape=[bf16(n, rounds * cols)] * (attn * group),
        in_specs=[VMEM] * (planes + group * attn),
        out_specs=[VMEM] * (attn * group),
        compiler_params=params(28),
        cost_estimate=LIGHT,
        name="project",
    )(*[blocks[i] for i in range(planes)], *everything)
    placed = [
        found[m * group + k] if m == k == 0 else across(found[m * group + k], k, m)
        for m, k in farthest_first(attn, group)
    ]

    if cols % HEAD == 0:
        return pl.pallas_call(
            functools.partial(place_kernel, group, attn, planes),
            out_shape=bf16(n, planes * group * cols),
            in_specs=[VMEM] * len(placed),
            out_specs=VMEM,
            name="place",
        )(*placed)
    out = jnp.zeros((n, planes * group * cols), jnp.bfloat16)
    for r in range(rounds):
        for (m, k), piece in zip(farthest_first(attn, group), placed):
            at = column_of(group, attn, planes, r, m, k, cols)
            out = lax.dynamic_update_slice_in_dim(out, piece[:, r * cols : (r + 1) * cols], at, 1)
    return out


def solution(mesh):
    return jax.shard_map(
        functools.partial(shards, mesh.shape["dense"], mesh.shape["attn"]),
        mesh=mesh,
        in_specs=(
            P("dense", "attn"),
            P("dense", "attn"),
            P("dense", "attn"),
            P(),
            P("attn", "dense"),
        ),
        out_specs=P("dense", "attn"),
        check_vma=False,
    )
```

```python
import functools
import math

import jax
import jax.numpy as jnp
from jax import lax
from jax.experimental import pallas as pl
from jax.experimental.pallas import tpu as pltpu
from jax.sharding import PartitionSpec as P

HEAD = 128
NEGATIVE = -1e30
AXES = ("dense", "attn")
ANY = pl.BlockSpec(memory_space=pl.ANY)
SMEM = pl.BlockSpec(memory_space=pltpu.SMEM)
VMEM = pl.BlockSpec(memory_space=pltpu.VMEM)
LIGHT = pl.CostEstimate(flops=0, bytes_accessed=0, transcendentals=0)


def xor(a, b):
    return lax.bitwise_xor(a, jnp.int32(b))


def params(mib):
    return pltpu.CompilerParams(vmem_limit_bytes=mib * 2**20)


def place_in(group):
    device = lax.axis_index("dense").astype(jnp.int32)
    return device // group, lax.rem(device, jnp.int32(group)), lax.axis_index("attn").astype(jnp.int32)


def turn_of(z, y, planes, attn):
    return lax.bitwise_xor(z // (planes // attn), y)


def split_kv_kernel(group, *refs):
    g = place_in(group)[1]
    for core in range(2):
        k_ref, v_ref = refs[2 * core : 2 * core + 2]
        for o, out in enumerate(refs[4:]):
            at = pl.ds(pl.multiple_of(xor(g, 2 * o) * HEAD, HEAD), HEAD)
            out[core, :, :HEAD] = k_ref[:, at]
            out[core, :, HEAD:] = v_ref[:, at]


def split_q_kernel(group, *refs):
    g = place_in(group)[1]
    width = refs[2].shape[2]
    for core in range(2):
        for o, out in enumerate(refs[2:]):
            out[core] = refs[core][:, pl.ds(pl.multiple_of(xor(g, 2 * o) * width, width), width)]


def split_w_kernel(group, w_ref, *outs):
    g, y = place_in(group)[1:]
    rows, cols = outs[0].shape
    width = rows // group
    for m, out in enumerate(outs):
        at = pl.ds(pl.multiple_of(xor(y, m) * cols, cols), cols)
        for j in range(group):
            part = w_ref[pl.ds(pl.multiple_of(xor(g, j) * width, width), width), at]
            out[j * width : (j + 1) * width, :] = part


def attention_kernel(group, heads, back, pairs, carried, final, seg_ref, segrow_ref, *refs):
    n_kv, n_q = len(back) * group, len(pairs) * 2
    refs = list(refs)
    take = lambda count: [refs.pop(0) for _ in range(count)]
    q_refs, kv_refs = take(len(pairs)), take(n_kv // 2)
    state_refs = [take(2) for _ in pairs] if carried else None
    out_refs = take(1 if final else 2)
    q_s, k_s, v_s, m_own, acc_own, seg_s, sem = refs
    unit = k_s.shape[1] // segrow_ref.shape[1]
    n = segrow_ref.shape[1]
    rows = heads * n
    lanes = n // HEAD
    copies = []
    for k in range(n_q):
        for h in range(heads):
            q_part = q_refs[k // 2].at[k % 2, :, pl.ds(h * HEAD, HEAD)]
            copies.append((q_part, q_s.at[k, pl.ds(h * n, n), :]))
    for i in range(n_kv):
        kv = kv_refs[i // 2].at[i % 2]
        at = pl.ds(i % unit * n, n)
        copies.append((kv.at[:, pl.ds(0, HEAD)], k_s.at[i // unit, at, :]))
        copies.append((kv.at[:, pl.ds(HEAD, HEAD)], v_s.at[i // unit, at, pl.ds(0, HEAD)]))
    copies = [pltpu.make_async_copy(a, b, sem.at[i]) for i, (a, b) in enumerate(copies)]
    for c in copies:
        c.start()
    v_s[:, :, HEAD:] = jnp.ones((n_kv // unit, unit * n, HEAD), jnp.bfloat16)
    for c in copies:
        c.wait()

    plane, g, _ = place_in(group)
    scale = math.log2(math.e) / math.sqrt(HEAD)

    def one_query_piece(pair, core, carry):
        at = 2 * pair + core
        given = [ref.at[core] for ref in state_refs[pair]] if carried else None
        m_s, acc_s = (m_own, acc_own) if final else (ref.at[at] for ref in out_refs)
        qp = plane * group + lax.bitwise_xor(g, 2 * pairs[pair] + core)
        q_first, q_last = seg_ref[qp * n], seg_ref[qp * n + n - 1]

        def piece(i, which):
            i = i * unit + which
            kp = (plane - back[0] - i // group) * group + lax.bitwise_xor(g, lax.rem(i, group))
            safe = jnp.maximum(kp, 0)
            active = (kp >= 0) & (kp <= qp) & (seg_ref[safe * n + n - 1] >= q_first)
            whole = (kp >= 0) & (kp < qp) & (seg_ref[safe * n] == q_last)
            return kp, safe, active, whole

        def needed(i):
            return functools.reduce(jnp.logical_or, [piece(i, which)[2] for which in range(unit)])

        def mix(i, carry):
            pieces = [piece(i, which) for which in range(unit)]
            active = needed(i)
            whole = functools.reduce(jnp.logical_and, [p[3] for p in pieces])

            def scores(h):
                return lax.dot_general(
                    q_s[at, h * n : (h + 1) * n],
                    k_s[i],
                    (((1,), (1,)), ((), ())),
                    preferred_element_type=jnp.float32,
                )

            def each_head(seen):
                ahead = scores(0)
                for h in range(heads):
                    s, ahead = ahead, scores(h + 1) if h + 1 < heads else None
                    head(h, s, seen)

            def head(h, s, seen):
                row = slice(h * n, (h + 1) * n)
                if seen is not None:
                    s = jnp.where(seen, s, NEGATIVE)
                old = m_s[row]
                top = jnp.maximum(old, jnp.max(s, axis=1, keepdims=True))
                m_s[row] = top
                shrink = jnp.exp2((old - top) * scale)
                top = jnp.concatenate([top] * (unit * lanes), axis=1)
                weights = jnp.exp2((s - top) * scale).astype(jnp.bfloat16)
                found = jnp.dot(weights, v_s[i], preferred_element_type=jnp.float32)
                acc_s[row] = acc_s[row] * jnp.concatenate([shrink] * 2, axis=1) + found

            @pl.when(active & whole)
            def _():
                each_head(None)

            @pl.when(active & jnp.logical_not(whole))
            def _():
                ahead = lax.broadcasted_iota(jnp.int32, (n, HEAD), 1) - lax.broadcasted_iota(
                    jnp.int32, (n, HEAD), 0
                )
                seen = []
                for kp, safe, _, _ in pieces:
                    seg_k = segrow_ref[pl.ds(safe, 1), :].astype(jnp.float32)
                    for t in range(lanes):
                        same = seg_s[...] == seg_k[:, t * HEAD : (t + 1) * HEAD]
                        seen.append(same & (ahead + t * HEAD <= (qp - kp) * n) & (kp >= 0))
                seen = jnp.concatenate(seen, axis=1)
                each_head(seen)

            return carry

        def give(summed):
            for h in range(heads):
                row = slice(h * n, (h + 1) * n)
                out_refs[0][at, :, h * HEAD : (h + 1) * HEAD] = (
                    summed[row, :HEAD] / summed[row, HEAD:]
                ).astype(jnp.bfloat16)

        def all_keys():
            seg_row = segrow_ref[pl.ds(qp, 1), :].astype(jnp.float32)
            seg_s[...] = jnp.broadcast_to(seg_row, (HEAD, n)).T
            if carried:
                m_s[...] = given[0][...]
                acc_s[...] = given[1][...]
            else:
                m_s[...] = jnp.full(m_s.shape, NEGATIVE, jnp.float32)
                acc_s[...] = jnp.zeros(acc_s.shape, jnp.float32)
            lax.fori_loop(0, n_kv // unit, mix, 0)

        if carried:
            any_needed = lax.fori_loop(
                0, n_kv // unit, lambda i, seen: seen | needed(i).astype(jnp.int32), jnp.int32(0)
            )

            @pl.when(any_needed > 0)
            def _():
                all_keys()
                give(acc_s)

            @pl.when(any_needed == 0)
            def _():
                give(given[1])
        else:
            all_keys()
            if final:
                give(acc_s)
        return carry

    for pair in range(len(pairs)):
        lax.fori_loop(0, 2, functools.partial(one_query_piece, pair), 0)


def attention(group, heads, back, pairs, segments, q, kv, carried=None, final=True):
    n, width = q[0].shape[1:]
    rows, n_kv, n_q = heads * n, 2 * len(kv), 2 * len(pairs)
    if final:
        out_shape = [jax.ShapeDtypeStruct((n_q, n, width), jnp.bfloat16)]
    else:
        out_shape = [jax.ShapeDtypeStruct((n_q, rows, lanes), jnp.float32) for lanes in (HEAD, 2 * HEAD)]
    carried = list(carried or ())
    unit = 1 if carried else 2
    found = pl.pallas_call(
        functools.partial(attention_kernel, group, heads, back, pairs, bool(carried), final),
        out_shape=out_shape,
        in_specs=[SMEM, VMEM] + [ANY] * (len(q) + len(kv)) + [VMEM] * len(carried),
        out_specs=[VMEM] * len(out_shape),
        scratch_shapes=[
            pltpu.VMEM((n_q, rows, HEAD), jnp.bfloat16),
            pltpu.VMEM((n_kv // unit, unit * n, HEAD), jnp.bfloat16),
            pltpu.VMEM((n_kv // unit, unit * n, 2 * HEAD), jnp.bfloat16),
            pltpu.VMEM((rows, HEAD), jnp.float32),
            pltpu.VMEM((rows, 2 * HEAD), jnp.float32),
            pltpu.VMEM((n, HEAD), jnp.float32),
            pltpu.SemaphoreType.DMA((n_q * heads + 2 * n_kv,)),
        ],
        compiler_params=params(28),
        cost_estimate=LIGHT,
        name="attention",
    )(segments, segments.reshape(-1, n), *q, *kv, *carried)
    return found[0] if final else found


def project_kernel(group, attn, planes, *refs):
    refs = list(refs)
    take = lambda count: [refs.pop(0) for _ in range(count)]
    w_refs, a_refs, out_refs = take(planes), take(group * attn), take(group * attn)
    z, _, y = place_in(group)
    cols = w_refs[0].shape[1]
    rounds = planes // attn
    turn = turn_of(z, y, planes, attn)
    for k in range(group):
        rows = jnp.concatenate([a_refs[i][(i % group) ^ k] for i in range(attn * group)], axis=1)
        dot = lambda weights: jnp.dot(rows, weights, preferred_element_type=jnp.float32).astype(jnp.bfloat16)
        if cols % HEAD == 0:
            found = dot(jnp.concatenate([w_ref[...] for w_ref in w_refs], axis=1))
            found = [found[:, t * rounds * cols : (t + 1) * rounds * cols] for t in range(attn)]
        else:
            found = [
                jnp.concatenate([dot(w_ref[...]) for w_ref in w_refs[t * rounds : (t + 1) * rounds]], axis=1)
                for t in range(attn)
            ]
        for to in range(attn):
            here = xor(turn, to)
            mine = found[0]
            for t in range(1, attn):
                mine = jnp.where(here == t, found[t], mine)
            out_refs[to * group + k][...] = mine


def farthest_first(attn, group):
    return sorted(((m, k) for m in range(attn) for k in range(group)), key=lambda at: (at[1] > 1, at[0] > 0, at[1]))[
        ::-1
    ]


def column_of(group, attn, planes, r, m, k, cols):
    z, g, y = place_in(group)
    rounds = planes // attn
    return ((xor(lax.rem(z, jnp.int32(rounds)), r) * group + xor(g, k)) * attn + xor(y, m)) * cols


def place_kernel(group, attn, planes, *refs):
    out_ref = refs[-1]
    rounds = planes // attn
    cols = refs[0].shape[1] // rounds
    for r in range(rounds):
        for (m, k), ref in zip(farthest_first(attn, group), refs):
            at = pl.multiple_of(column_of(group, attn, planes, r, m, k, cols), cols)
            out_ref[:, pl.ds(at, cols)] = ref[:, r * cols : (r + 1) * cols]


def shards(dense, attn, queries, keys, values, segments, out_weight):
    n = queries.shape[0]
    tokens = segments.shape[0]
    group = keys.shape[1] // HEAD
    heads = queries.shape[1] // HEAD // group
    width = heads * HEAD
    planes = dense // group
    rounds = planes // attn
    hops = min(-(-(tokens // 2 - 1) // (n * group)), planes - 1)
    cols = out_weight.shape[1] // attn
    bf16 = lambda *shape: jax.ShapeDtypeStruct(shape, jnp.bfloat16)

    def number(z, g, y):
        return (z * group + g) * attn + y

    def pairs(move):
        found = []
        for z in range(planes):
            for g in range(group):
                for y in range(attn):
                    to = move(z, g, y)
                    if 0 <= to[0] < planes:
                        found.append((number(z, g, y), number(*to)))
        return found

    def across(array, j, m):
        with jax.named_scope(f"across_{j}_{m}"):
            return lax.ppermute(array, AXES, pairs(lambda z, g, y: (z, g ^ j, y ^ m)))

    def up(array, j=0):
        with jax.named_scope(f"up_{j}"):
            return lax.ppermute(array, AXES, pairs(lambda z, g, y: (z + 1, g ^ j, y)))

    def between(array, i):
        with jax.named_scope(f"between_{i}"):
            return lax.ppermute(array, AXES, pairs(lambda z, g, y: (z ^ i, g, y)))

    def with_other_core(arrays):
        return [which for array in arrays for which in (array, across(array, 1, 0))]

    after = lambda array, *others: lax.optimization_barrier((array, *others))

    if cols % HEAD == 0:
        own = pl.pallas_call(
            functools.partial(split_w_kernel, group),
            out_shape=[bf16(out_weight.shape[0], cols)] * attn,
            in_specs=[VMEM],
            out_specs=[VMEM] * attn,
            name="split_w",
        )(out_weight)
    else:
        _, g, y = place_in(group)
        ordered = jnp.concatenate(
            [lax.dynamic_slice_in_dim(out_weight, xor(g, j) * width, width, 0) for j in range(group)]
        )
        own = [lax.dynamic_slice_in_dim(ordered, xor(y, m) * cols, cols, 1) for m in range(attn)]
    others = [own[0]] + [across(own[m], 0, m) for m in range(1, attn)]

    keys, *own = after(keys, *own)
    kv = pl.pallas_call(
        functools.partial(split_kv_kernel, group),
        out_shape=[bf16(2, n, 2 * HEAD)] * (group // 2),
        in_specs=[VMEM] * 4,
        out_specs=[VMEM] * (group // 2),
        name="split_kv",
    )(keys, values, across(keys, 1, 0), across(values, 1, 0))
    links = [[kv[0]] + [across(kv[o], 2 * o, 0) for o in range(1, group // 2)]]
    links.append([up(kv[o], 2 * o) for o in range(group // 2)])

    queries, far_queries, *others = after(queries, across(queries, 1, 0), *others)
    q = pl.pallas_call(
        functools.partial(split_q_kernel, group),
        out_shape=[bf16(2, n, width)] * (group // 2),
        in_specs=[VMEM] * 2,
        out_specs=[VMEM] * (group // 2),
        name="split_q",
    )(queries, far_queries)
    q = [q[0]] + [across(q[o], 2 * o, 0) for o in range(1, group // 2)]

    own = jnp.concatenate(others)
    own, links[1][-1] = after(own, links[1][-1])
    for _ in range(1, hops):
        links.append([up(pair) for pair in links[-1]])
    blocks = {0: own, planes // 2: between(own, planes // 2), planes // 4: between(own, planes // 4)}

    near = [pair for pairs_of in links[:hops] for pair in pairs_of]
    carried = []
    for o in range(group // 2):
        carried += attention(group, heads, range(hops), [o], segments, [q[o]], near, final=False)
    attended = attention(
        group, heads, range(hops, hops + 1), range(group // 2), segments, q, links[hops], carried
    )

    everything = []
    for m in range(attn):
        everything += with_other_core(
            [attended if o == m == 0 else across(attended, 2 * o, m) for o in range(group // 2)]
        )

    stride = planes // 2
    while stride:
        for i in range(0, planes, 2 * stride):
            if i + stride not in blocks:
                blocks[i + stride] = between(blocks[i], stride)
        stride //= 2

    found = pl.pallas_call(
        functools.partial(project_kernel, group, attn, planes),
        out_shape=[bf16(n, rounds * cols)] * (attn * group),
        in_specs=[VMEM] * (planes + group * attn),
        out_specs=[VMEM] * (attn * group),
        compiler_params=params(28),
        cost_estimate=LIGHT,
        name="project",
    )(*[blocks[i] for i in range(planes)], *everything)
    placed = [
        found[m * group + k] if m == k == 0 else across(found[m * group + k], k, m)
        for m, k in farthest_first(attn, group)
    ]

    if cols % HEAD == 0:
        return pl.pallas_call(
            functools.partial(place_kernel, group, attn, planes),
            out_shape=bf16(n, planes * group * cols),
            in_specs=[VMEM] * len(placed),
            out_specs=VMEM,
            name="place",
        )(*placed)
    out = jnp.zeros((n, planes * group * cols), jnp.bfloat16)
    for r in range(rounds):
        for (m, k), piece in zip(farthest_first(attn, group), placed):
            at = column_of(group, attn, planes, r, m, k, cols)
            out = lax.dynamic_update_slice_in_dim(out, piece[:, r * cols : (r + 1) * cols], at, 1)
    return out


def solution(mesh):
    return jax.shard_map(
        functools.partial(shards, mesh.shape["dense"], mesh.shape["attn"]),
        mesh=mesh,
        in_specs=(
            P("dense", "attn"),
            P("dense", "attn"),
            P("dense", "attn"),
            P(),
            P("attn", "dense"),
        ),
        out_specs=P("dense", "attn"),
        check_vma=False,
    )
```

```python
import functools
import math

import jax
import jax.numpy as jnp
from jax import lax
from jax.experimental import pallas as pl
from jax.experimental.pallas import tpu as pltpu
from jax.sharding import PartitionSpec as P

HEAD = 128
NEGATIVE = -1e30
AXES = ("dense", "attn")
ANY = pl.BlockSpec(memory_space=pl.ANY)
SMEM = pl.BlockSpec(memory_space=pltpu.SMEM)
VMEM = pl.BlockSpec(memory_space=pltpu.VMEM)
LIGHT = pl.CostEstimate(flops=0, bytes_accessed=0, transcendentals=0)


def xor(a, b):
    return lax.bitwise_xor(a, jnp.int32(b))


def params(mib):
    return pltpu.CompilerParams(vmem_limit_bytes=mib * 2**20)


def place_in(group):
    device = lax.axis_index("dense").astype(jnp.int32)
    return device // group, lax.rem(device, jnp.int32(group)), lax.axis_index("attn").astype(jnp.int32)


def turn_of(z, y, planes, attn):
    return lax.bitwise_xor(z // (planes // attn), y)


def split_kv_kernel(group, *refs):
    g = place_in(group)[1]
    for core in range(2):
        k_ref, v_ref = refs[2 * core : 2 * core + 2]
        for o, out in enumerate(refs[4:]):
            at = pl.ds(pl.multiple_of(xor(g, 2 * o) * HEAD, HEAD), HEAD)
            out[core, :, :HEAD] = k_ref[:, at]
            out[core, :, HEAD:] = v_ref[:, at]


def split_q_kernel(group, *refs):
    g = place_in(group)[1]
    width = refs[2].shape[2]
    for core in range(2):
        for o, out in enumerate(refs[2:]):
            out[core] = refs[core][:, pl.ds(pl.multiple_of(xor(g, 2 * o) * width, width), width)]


def split_w_kernel(group, w_ref, *outs):
    g, y = place_in(group)[1:]
    rows, cols = outs[0].shape
    width = rows // group
    for m, out in enumerate(outs):
        at = pl.ds(pl.multiple_of(xor(y, m) * cols, cols), cols)
        for j in range(group):
            part = w_ref[pl.ds(pl.multiple_of(xor(g, j) * width, width), width), at]
            out[j * width : (j + 1) * width, :] = part


def attention_kernel(group, heads, back, pairs, carried, final, seg_ref, segrow_ref, *refs):
    n_kv, n_q = len(back) * group, len(pairs) * 2
    refs = list(refs)
    take = lambda count: [refs.pop(0) for _ in range(count)]
    q_refs, kv_refs = take(len(pairs)), take(n_kv // 2)
    state_refs = [take(2) for _ in pairs] if carried else None
    out_refs = take(1 if final else 2)
    q_s, k_s, v_s, m_own, acc_own, seg_s, sem = refs
    unit = k_s.shape[1] // segrow_ref.shape[1]
    n = segrow_ref.shape[1]
    rows = heads * n
    lanes = n // HEAD
    copies = []
    for k in range(n_q):
        for h in range(heads):
            q_part = q_refs[k // 2].at[k % 2, :, pl.ds(h * HEAD, HEAD)]
            copies.append((q_part, q_s.at[k, pl.ds(h * n, n), :]))
    for i in range(n_kv):
        kv = kv_refs[i // 2].at[i % 2]
        at = pl.ds(i % unit * n, n)
        copies.append((kv.at[:, pl.ds(0, HEAD)], k_s.at[i // unit, at, :]))
        copies.append((kv.at[:, pl.ds(HEAD, HEAD)], v_s.at[i // unit, at, pl.ds(0, HEAD)]))
    copies = [pltpu.make_async_copy(a, b, sem.at[i]) for i, (a, b) in enumerate(copies)]
    for c in copies:
        c.start()
    v_s[:, :, HEAD:] = jnp.ones((n_kv // unit, unit * n, HEAD), jnp.bfloat16)
    for c in copies:
        c.wait()

    plane, g, _ = place_in(group)
    scale = math.log2(math.e) / math.sqrt(HEAD)

    def one_query_piece(pair, core, carry):
        at = 2 * pair + core
        given = [ref.at[core] for ref in state_refs[pair]] if carried else None
        m_s, acc_s = (m_own, acc_own) if final else (ref.at[at] for ref in out_refs)
        qp = plane * group + lax.bitwise_xor(g, 2 * pairs[pair] + core)
        q_first, q_last = seg_ref[qp * n], seg_ref[qp * n + n - 1]

        def piece(i, which):
            i = i * unit + which
            kp = (plane - back[0] - i // group) * group + lax.bitwise_xor(g, lax.rem(i, group))
            safe = jnp.maximum(kp, 0)
            active = (kp >= 0) & (kp <= qp) & (seg_ref[safe * n + n - 1] >= q_first)
            whole = (kp >= 0) & (kp < qp) & (seg_ref[safe * n] == q_last)
            return kp, safe, active, whole

        def needed(i):
            return functools.reduce(jnp.logical_or, [piece(i, which)[2] for which in range(unit)])

        def mix(i, carry):
            pieces = [piece(i, which) for which in range(unit)]
            active = needed(i)
            whole = functools.reduce(jnp.logical_and, [p[3] for p in pieces])

            def scores(h):
                return lax.dot_general(
                    q_s[at, h * n : (h + 1) * n],
                    k_s[i],
                    (((1,), (1,)), ((), ())),
                    preferred_element_type=jnp.float32,
                )

            def each_head(seen):
                ahead = scores(0)
                for h in range(heads):
                    s, ahead = ahead, scores(h + 1) if h + 1 < heads else None
                    head(h, s, seen)

            def head(h, s, seen):
                row = slice(h * n, (h + 1) * n)
                if seen is not None:
                    s = jnp.where(seen, s, NEGATIVE)
                old = m_s[row]
                top = jnp.maximum(old, jnp.max(s, axis=1, keepdims=True))
                m_s[row] = top
                shrink = jnp.exp2((old - top) * scale)
                top = jnp.concatenate([top] * (unit * lanes), axis=1)
                weights = jnp.exp2((s - top) * scale).astype(jnp.bfloat16)
                found = jnp.dot(weights, v_s[i], preferred_element_type=jnp.float32)
                acc_s[row] = acc_s[row] * jnp.concatenate([shrink] * 2, axis=1) + found

            @pl.when(active & whole)
            def _():
                each_head(None)

            @pl.when(active & jnp.logical_not(whole))
            def _():
                ahead = lax.broadcasted_iota(jnp.int32, (n, HEAD), 1) - lax.broadcasted_iota(
                    jnp.int32, (n, HEAD), 0
                )
                seen = []
                for kp, safe, _, _ in pieces:
                    seg_k = segrow_ref[pl.ds(safe, 1), :].astype(jnp.float32)
                    for t in range(lanes):
                        same = seg_s[...] == seg_k[:, t * HEAD : (t + 1) * HEAD]
                        seen.append(same & (ahead + t * HEAD <= (qp - kp) * n) & (kp >= 0))
                seen = jnp.concatenate(seen, axis=1)
                each_head(seen)

            return carry

        def give(summed):
            for h in range(heads):
                row = slice(h * n, (h + 1) * n)
                out_refs[0][at, :, h * HEAD : (h + 1) * HEAD] = (
                    summed[row, :HEAD] / summed[row, HEAD:]
                ).astype(jnp.bfloat16)

        def all_keys():
            seg_row = segrow_ref[pl.ds(qp, 1), :].astype(jnp.float32)
            seg_s[...] = jnp.broadcast_to(seg_row, (HEAD, n)).T
            if carried:
                m_s[...] = given[0][...]
                acc_s[...] = given[1][...]
            else:
                m_s[...] = jnp.full(m_s.shape, NEGATIVE, jnp.float32)
                acc_s[...] = jnp.zeros(acc_s.shape, jnp.float32)
            lax.fori_loop(0, n_kv // unit, mix, 0)

        if carried:
            any_needed = lax.fori_loop(
                0, n_kv // unit, lambda i, seen: seen | needed(i).astype(jnp.int32), jnp.int32(0)
            )

            @pl.when(any_needed > 0)
            def _():
                all_keys()
                give(acc_s)

            @pl.when(any_needed == 0)
            def _():
                give(given[1])
        else:
            all_keys()
            if final:
                give(acc_s)
        return carry

    for pair in range(len(pairs)):
        lax.fori_loop(0, 2, functools.partial(one_query_piece, pair), 0)


def attention(group, heads, back, pairs, segments, q, kv, carried=None, final=True):
    n, width = q[0].shape[1:]
    rows, n_kv, n_q = heads * n, 2 * len(kv), 2 * len(pairs)
    if final:
        out_shape = [jax.ShapeDtypeStruct((n_q, n, width), jnp.bfloat16)]
    else:
        out_shape = [jax.ShapeDtypeStruct((n_q, rows, lanes), jnp.float32) for lanes in (HEAD, 2 * HEAD)]
    carried = list(carried or ())
    unit = 1 if carried else 2
    found = pl.pallas_call(
        functools.partial(attention_kernel, group, heads, back, pairs, bool(carried), final),
        out_shape=out_shape,
        in_specs=[SMEM, VMEM] + [ANY] * (len(q) + len(kv)) + [VMEM] * len(carried),
        out_specs=[VMEM] * len(out_shape),
        scratch_shapes=[
            pltpu.VMEM((n_q, rows, HEAD), jnp.bfloat16),
            pltpu.VMEM((n_kv // unit, unit * n, HEAD), jnp.bfloat16),
            pltpu.VMEM((n_kv // unit, unit * n, 2 * HEAD), jnp.bfloat16),
            pltpu.VMEM((rows, HEAD), jnp.float32),
            pltpu.VMEM((rows, 2 * HEAD), jnp.float32),
            pltpu.VMEM((n, HEAD), jnp.float32),
            pltpu.SemaphoreType.DMA((n_q * heads + 2 * n_kv,)),
        ],
        compiler_params=params(28),
        cost_estimate=LIGHT,
        name="attention",
    )(segments, segments.reshape(-1, n), *q, *kv, *carried)
    return found[0] if final else found


def project_kernel(group, attn, planes, *refs):
    refs = list(refs)
    take = lambda count: [refs.pop(0) for _ in range(count)]
    w_refs, a_refs, out_refs = take(planes), take(group * attn), take(group * attn)
    z, _, y = place_in(group)
    cols = w_refs[0].shape[1]
    rounds = planes // attn
    turn = turn_of(z, y, planes, attn)
    for k in range(group):
        rows = jnp.concatenate([a_refs[i][(i % group) ^ k] for i in range(attn * group)], axis=1)
        dot = lambda weights: jnp.dot(rows, weights, preferred_element_type=jnp.float32).astype(jnp.bfloat16)
        if cols % HEAD == 0:
            found = dot(jnp.concatenate([w_ref[...] for w_ref in w_refs], axis=1))
            found = [found[:, t * rounds * cols : (t + 1) * rounds * cols] for t in range(attn)]
        else:
            found = [
                jnp.concatenate([dot(w_ref[...]) for w_ref in w_refs[t * rounds : (t + 1) * rounds]], axis=1)
                for t in range(attn)
            ]
        for to in range(attn):
            here = xor(turn, to)
            mine = found[0]
            for t in range(1, attn):
                mine = jnp.where(here == t, found[t], mine)
            out_refs[to * group + k][...] = mine


def farthest_first(attn, group):
    return sorted(((m, k) for m in range(attn) for k in range(group)), key=lambda at: (at[1] > 1, at[0] > 0, at[1]))[
        ::-1
    ]


def column_of(group, attn, planes, r, m, k, cols):
    z, g, y = place_in(group)
    rounds = planes // attn
    return ((xor(lax.rem(z, jnp.int32(rounds)), r) * group + xor(g, k)) * attn + xor(y, m)) * cols


def place_kernel(group, attn, planes, *refs):
    out_ref = refs[-1]
    rounds = planes // attn
    cols = refs[0].shape[1] // rounds
    for r in range(rounds):
        for (m, k), ref in zip(farthest_first(attn, group), refs):
            at = pl.multiple_of(column_of(group, attn, planes, r, m, k, cols), cols)
            out_ref[:, pl.ds(at, cols)] = ref[:, r * cols : (r + 1) * cols]


def shards(dense, attn, queries, keys, values, segments, out_weight):
    n = queries.shape[0]
    tokens = segments.shape[0]
    group = keys.shape[1] // HEAD
    heads = queries.shape[1] // HEAD // group
    width = heads * HEAD
    planes = dense // group
    rounds = planes // attn
    hops = min(-(-(tokens // 2 - 1) // (n * group)), planes - 1)
    cols = out_weight.shape[1] // attn
    bf16 = lambda *shape: jax.ShapeDtypeStruct(shape, jnp.bfloat16)

    def number(z, g, y):
        return (z * group + g) * attn + y

    def pairs(move):
        found = []
        for z in range(planes):
            for g in range(group):
                for y in range(attn):
                    to = move(z, g, y)
                    if 0 <= to[0] < planes:
                        found.append((number(z, g, y), number(*to)))
        return found

    def across(array, j, m):
        with jax.named_scope(f"across_{j}_{m}"):
            return lax.ppermute(array, AXES, pairs(lambda z, g, y: (z, g ^ j, y ^ m)))

    def up(array, j=0):
        with jax.named_scope(f"up_{j}"):
            return lax.ppermute(array, AXES, pairs(lambda z, g, y: (z + 1, g ^ j, y)))

    def between(array, i):
        with jax.named_scope(f"between_{i}"):
            return lax.ppermute(array, AXES, pairs(lambda z, g, y: (z ^ i, g, y)))

    def with_other_core(arrays):
        return [which for array in arrays for which in (array, across(array, 1, 0))]

    after = lambda array, *others: lax.optimization_barrier((array, *others))

    if cols % HEAD == 0:
        own = pl.pallas_call(
            functools.partial(split_w_kernel, group),
            out_shape=[bf16(out_weight.shape[0], cols)] * attn,
            in_specs=[VMEM],
            out_specs=[VMEM] * attn,
            name="split_w",
        )(out_weight)
    else:
        _, g, y = place_in(group)
        ordered = jnp.concatenate(
            [lax.dynamic_slice_in_dim(out_weight, xor(g, j) * width, width, 0) for j in range(group)]
        )
        own = [lax.dynamic_slice_in_dim(ordered, xor(y, m) * cols, cols, 1) for m in range(attn)]
    others = [own[0]] + [across(own[m], 0, m) for m in range(1, attn)]

    keys, *own = after(keys, *own)
    kv = pl.pallas_call(
        functools.partial(split_kv_kernel, group),
        out_shape=[bf16(2, n, 2 * HEAD)] * (group // 2),
        in_specs=[VMEM] * 4,
        out_specs=[VMEM] * (group // 2),
        compiler_params=params(60),
        name="split_kv",
    )(keys, values, across(keys, 1, 0), across(values, 1, 0))
    links = [[kv[0]] + [across(kv[o], 2 * o, 0) for o in range(1, group // 2)]]
    links.append([up(kv[o], 2 * o) for o in range(group // 2)])

    queries, far_queries, *others = after(queries, across(queries, 1, 0), *others)
    q = pl.pallas_call(
        functools.partial(split_q_kernel, group),
        out_shape=[bf16(2, n, width)] * (group // 2),
        in_specs=[VMEM] * 2,
        out_specs=[VMEM] * (group // 2),
        compiler_params=params(60),
        name="split_q",
    )(queries, far_queries)
    q = [q[0]] + [across(q[o], 2 * o, 0) for o in range(1, group // 2)]

    own = jnp.concatenate(others)
    own, links[1][-1] = after(own, links[1][-1])
    for _ in range(1, hops):
        links.append([up(pair) for pair in links[-1]])
    blocks = {0: own, planes // 2: between(own, planes // 2), planes // 4: between(own, planes // 4)}

    near = [pair for pairs_of in links[:hops] for pair in pairs_of]
    carried = []
    for o in range(group // 2):
        carried += attention(group, heads, range(hops), [o], segments, [q[o]], near, final=False)
    attended = attention(
        group, heads, range(hops, hops + 1), range(group // 2), segments, q, links[hops], carried
    )

    everything = []
    for m in range(attn):
        everything += with_other_core(
            [attended if o == m == 0 else across(attended, 2 * o, m) for o in range(group // 2)]
        )

    stride = planes // 2
    while stride:
        for i in range(0, planes, 2 * stride):
            if i + stride not in blocks:
                blocks[i + stride] = between(blocks[i], stride)
        stride //= 2

    found = pl.pallas_call(
        functools.partial(project_kernel, group, attn, planes),
        out_shape=[bf16(n, rounds * cols)] * (attn * group),
        in_specs=[VMEM] * (planes + group * attn),
        out_specs=[VMEM] * (attn * group),
        compiler_params=params(28),
        cost_estimate=LIGHT,
        name="project",
    )(*[blocks[i] for i in range(planes)], *everything)
    placed = [
        found[m * group + k] if m == k == 0 else across(found[m * group + k], k, m)
        for m, k in farthest_first(attn, group)
    ]

    if cols % HEAD == 0:
        return pl.pallas_call(
            functools.partial(place_kernel, group, attn, planes),
            out_shape=bf16(n, planes * group * cols),
            in_specs=[VMEM] * len(placed),
            out_specs=VMEM,
            name="place",
        )(*placed)
    out = jnp.zeros((n, planes * group * cols), jnp.bfloat16)
    for r in range(rounds):
        for (m, k), piece in zip(farthest_first(attn, group), placed):
            at = column_of(group, attn, planes, r, m, k, cols)
            out = lax.dynamic_update_slice_in_dim(out, piece[:, r * cols : (r + 1) * cols], at, 1)
    return out


def solution(mesh):
    return jax.shard_map(
        functools.partial(shards, mesh.shape["dense"], mesh.shape["attn"]),
        mesh=mesh,
        in_specs=(
            P("dense", "attn"),
            P("dense", "attn"),
            P("dense", "attn"),
            P(),
            P("attn", "dense"),
        ),
        out_specs=P("dense", "attn"),
        check_vma=False,
    )
```
